128 devices in a mesh: tm: 4 (over y_hi, core), seq: 32 (over x, y_lo, z).
Axes of the slice: x: 4, y: 4 (y_hi: 2, y_lo: 2; y = y_hi * 2 + y_lo), z: 4, core: 2. Of those that a mesh axis runs over, the one named last changes fastest.
Arguments:
- trajectory: float32 [4, 1024, 5120], P('tm', 'seq'), may hold values from -6 to 6
- qkv_weight: bfloat16 [3, 5120, 4096], P(None, None, 'seq'), may hold values from -1 to 1
- out_weight: bfloat16 [4096, 5120], P('seq'), may hold values from -0.75 to 0.75
- shift_table: float32 [50, 5120], replicated, may hold values from -3 to 3
- scale_table: float32 [50, 5120], replicated, may hold values from -0.9 to 0.9
- gate_table: float32 [50, 5120], replicated, may hold values from 0.5 to 2
- step_sizes: float32 [50], replicated, may hold values from 0.1 to 0.5
- window_start: int32 [1], replicated, may hold values from 0 to 46
Outputs:
- new_trajectory: float32 [4, 1024, 5120], P('tm', 'seq')
The draws below stay inside these ranges and needn't reach their ends.
All inputs are finite; a program needn't handle non-finite values.
Results may differ from the reference program's by a relative error of at most 0.0056.
Values may be sent and summed in bfloat16 or wider, within the bound.
No kernel may reach another device: no remote copies, remote signals or barrier semaphores. Data moves between devices by JAX's collectives and lax.ppermute only.
A program may use at most 128 MiB of HBM per device.

```python
import math
import jax
import jax.numpy as jnp
from jax import lax

D = 5120
HEADS = 32
HDIM = 128
NSCHED = 50
HD = 4096
WINDOW = 4
TOKENS = 1024


def draw_qkv_weight(key, part):
    key = jax.random.fold_in(key, 11)
    key_q, key_k, key_v = jax.random.split(key, 3)
    base_q = jax.random.normal(key_q, (D, HEADS * HDIM), jnp.float32)
    base_v = jax.random.normal(key_v, (D, HEADS * HDIM), jnp.float32)
    base_k = jax.random.normal(key_k, (D, HEADS * HDIM), jnp.float32)
    query_part = base_q * (2.0 / D) ** 0.5
    key_part = base_k * (2.0 / D) ** 0.5
    value_part = base_v / D ** 0.5
    whole = jnp.stack([query_part, key_part, value_part], axis=0)
    return jnp.clip(whole, -1.0, 1.0).astype(jnp.bfloat16)


def block_scale(own_key, dims, shards, least, largest):
    def one(position, shards_of):
        heights = jax.random.uniform(jax.random.fold_in(jax.random.fold_in(own_key, 6), position), (shards_of,), jnp.float32, least / len(shards), largest / len(shards))
        return jnp.repeat(jnp.exp(heights), dims[position] // shards_of).reshape((-1,) + (1,) * (len(dims) - position - 1))

    loudness = one(*shards[0])
    for cut in shards[1:]:
        loudness = loudness * one(*cut)
    return loudness


def gaussian(key, extent, width, reach, cuts=(), kind=jnp.bfloat16):
    entries = width * jax.random.normal(key, extent, jnp.float32)
    if cuts:
        entries = entries * block_scale(key, extent, cuts, -0.22, 0.18)
    return jnp.clip(entries, -reach, reach).astype(kind)


def setup_inputs(seed: int = 0) -> dict:
    splits = jax.random.split(jax.random.key(seed), 9)
    trajectory = gaussian(splits[0], (WINDOW, TOKENS, D), 1.0, 6.0, ((0, 4), (1, 32)), jnp.float32)
    qkv_weight = draw_qkv_weight(jax.random.fold_in(splits[8], 71), 0)
    out_weight = gaussian(splits[2], (HD, D), (HD // 64) ** -0.5, 0.75, ((0, 32),))
    shift_table = gaussian(splits[3], (NSCHED, D), 0.5, 3.0, (), jnp.float32)
    scale_table = gaussian(splits[4], (NSCHED, D), 0.3, 0.9, (), jnp.float32)
    gate_table = jnp.clip(jnp.exp(jax.random.uniform(splits[5], (NSCHED, D), jnp.float32, math.log(0.5), math.log(2.0))), 0.5, 2.0)
    step_sizes = jnp.clip(jnp.exp(jax.random.uniform(splits[6], (NSCHED,), jnp.float32, math.log(0.1), math.log(0.5))), 0.1, 0.5)
    window_start = jax.random.randint(splits[7], (1,), 0, NSCHED - WINDOW + 1).astype(jnp.int32)
    return dict(trajectory=trajectory, qkv_weight=qkv_weight, out_weight=out_weight, shift_table=shift_table, scale_table=scale_table, gate_table=gate_table, step_sizes=step_sizes, window_start=window_start)


def attend_head(operands):
    queries, keys, values = operands
    scores = jnp.dot(queries, keys.T, preferred_element_type=jnp.float32) / math.sqrt(HDIM)
    top = lax.optimization_barrier(jnp.max(scores, axis=-1, keepdims=True))
    weights = jnp.exp(scores - top)
    probs = (weights / lax.optimization_barrier(jnp.sum(weights, axis=-1, keepdims=True))).astype(jnp.bfloat16)
    return jnp.dot(probs, values, preferred_element_type=jnp.float32).astype(jnp.bfloat16)

def reference(trajectory, qkv_weight, out_weight, shift_table, scale_table, gate_table, step_sizes, window_start):
    drifts = []
    for j in range(WINDOW):
        index = (window_start[0] + j).astype(jnp.int32)
        shift = lax.dynamic_slice_in_dim(shift_table, index, 1, 0)[0]
        scale = lax.dynamic_slice_in_dim(scale_table, index, 1, 0)[0]
        gate = lax.dynamic_slice_in_dim(gate_table, index, 1, 0)[0]
        step = lax.dynamic_slice_in_dim(step_sizes, index, 1, 0)[0]
        state = trajectory[j]
        normed = state * lax.rsqrt(lax.optimization_barrier(jnp.mean(state * state, axis=-1, keepdims=True)) + 1e-06)
        modulated = (normed * (1.0 + scale) + shift).astype(jnp.bfloat16)
        queries = jnp.dot(modulated, qkv_weight[0], preferred_element_type=jnp.float32).astype(jnp.bfloat16)
        keys = jnp.dot(modulated, qkv_weight[1], preferred_element_type=jnp.float32).astype(jnp.bfloat16)
        values = jnp.dot(modulated, qkv_weight[2], preferred_element_type=jnp.float32).astype(jnp.bfloat16)
        split_q = queries.reshape(TOKENS, HEADS, HDIM).transpose(1, 0, 2)
        split_k = keys.reshape(TOKENS, HEADS, HDIM).transpose(1, 0, 2)
        split_v = values.reshape(TOKENS, HEADS, HDIM).transpose(1, 0, 2)
        attended = lax.map(attend_head, (split_q, split_k, split_v))
        attended = attended.transpose(1, 0, 2).reshape(TOKENS, HEADS * HDIM)
        velocity = gate * jnp.dot(attended, out_weight, preferred_element_type=jnp.float32)
        drifts.append(step * velocity)
    summed = jnp.cumsum(jnp.stack(drifts, axis=0), axis=0)
    return trajectory[0][None] + summed
```

```python
import functools
import math

import jax
import jax.numpy as jnp
from jax import lax
from jax.experimental import pallas as pl
from jax.experimental.pallas import tpu as pltpu
from jax.sharding import PartitionSpec as P

HDIM = 128
XS, YLS, ZS = 4, 2, 4
BF16, F32 = jnp.bfloat16, jnp.float32
VMEM = pl.BlockSpec(memory_space=pltpu.VMEM)
SMEM = pl.BlockSpec(memory_space=pltpu.SMEM)
PARAMS = pltpu.CompilerParams(vmem_limit_bytes=56 * 1024 * 1024)


def moves(rule):
    pairs = []
    for yh in range(2):
        for core in range(2):
            for x in range(XS):
                for yl in range(YLS):
                    for z in range(ZS):
                        to = rule(yh, core, x, yl, z)
                        if to is not None:
                            pairs.append((flat(yh, core, x, yl, z), flat(*to)))
    return pairs


def flat(yh, core, x, yl, z):
    return (((yh * 2 + core) * XS + x) * YLS + yl) * ZS + z


def send(value, rule):
    return lax.ppermute(value, ("tm", "seq"), moves(rule))


def along_x(step):
    return lambda yh, core, x, yl, z: (yh, core, (x + step) % XS, yl, z)


def along_z(step):
    return lambda yh, core, x, yl, z: (yh, core, x, yl, (z + step) % ZS)


def to_other_core(yh, core, x, yl, z):
    return (yh, 1 - core, x, yl, z)


def to_partner(yh, core, x, yl, z):
    return (yh, core, x, 1 - yl, z)


def to_both_sides(yh, core, x, yl, z):
    return (yh if core == 0 else 1 - yh, core, x, 1 - yl, z)


def to_later_half(yh, core, x, yl, z):
    return (1, core, x, yl, z) if yh == 0 else None


def to_later_core(yh, core, x, yl, z):
    return (yh, 1, x, yl, z) if core == 0 else None


def modulate_kernel(index, state, scale, shift, out):
    row = index[0]
    value = state[...]
    mean = jnp.mean(value * value, axis=-1, keepdims=True)
    normed = value * lax.rsqrt(mean + 1e-06)
    out[...] = (normed * (1.0 + scale[pl.ds(row, 1), :]) + shift[pl.ds(row, 1), :]).astype(BF16)


def modulate(index, state, scale, shift):
    return pl.pallas_call(
        modulate_kernel,
        out_shape=jax.ShapeDtypeStruct(state.shape, BF16),
        in_specs=[SMEM, VMEM, VMEM, VMEM],
        out_specs=VMEM,
        compiler_params=PARAMS,
    )(index, state, scale, shift)


def project_kernel(count, chunk, *refs):
    core_ref, pieces, (own, mine, theirs), outs, total = (
        refs[0],
        refs[1 : 1 + count],
        refs[1 + count : 4 + count],
        refs[4 + count : 7 + count],
        refs[-1],
    )
    depth = own.shape[1]
    half = depth // 2
    first = core_ref[0] * half
    total[...] = jnp.zeros_like(total)

    def side(weight, start):
        def one(step, carry):
            at = pl.multiple_of(step * chunk, chunk)
            column = pl.multiple_of(start + at, 128)
            rows = jnp.concatenate([piece[:, pl.ds(column, chunk)] for piece in pieces], axis=0)
            for kind in range(3):
                both = jnp.concatenate(
                    [own[kind, pl.ds(column, chunk), :], weight[kind, pl.ds(at, chunk), :]], axis=-1
                )
                total[kind] += jnp.dot(rows, both, preferred_element_type=F32)
            return carry

        lax.fori_loop(0, half // chunk, one, 0)

    side(mine, first)
    side(theirs, half - first)
    for kind in range(3):
        outs[kind][...] = total[kind].astype(BF16)


def project(core, pieces, own, mine, theirs):
    tokens = sum(piece.shape[0] for piece in pieces)
    wide = 2 * HDIM
    return pl.pallas_call(
        functools.partial(project_kernel, len(pieces), 512),
        out_shape=[jax.ShapeDtypeStruct((tokens, wide), BF16)] * 3,
        in_specs=[SMEM] + [VMEM] * (len(pieces) + 3),
        out_specs=[VMEM] * 3,
        scratch_shapes=[pltpu.VMEM((3, tokens, wide), F32)],
        compiler_params=PARAMS,
    )(core, *pieces, own, mine, theirs)


def attend_kernel(cuts, queries, keys, values, far_keys, far_values, own, other, *refs):
    outs, attended = refs[:-1], refs[-1]
    scale = 1.0 / math.sqrt(HDIM)
    contract = (((1,), (1,)), ((), ()))
    tokens = queries.shape[0]
    rows = 256
    for head in range(2):
        here = slice(head * HDIM, (head + 1) * HDIM)
        there = slice((1 - head) * HDIM, (2 - head) * HDIM)
        all_keys = jnp.concatenate([keys[:, here], far_keys[:, there]], axis=0)
        all_values = jnp.concatenate([values[:, here], far_values[:, there]], axis=0)
        for start in range(0, tokens, rows):
            scores = lax.dot_general(
                queries[start : start + rows, here], all_keys, contract, preferred_element_type=F32
            )
            top = jnp.max(scores, axis=-1, keepdims=True)
            weights = jnp.exp((scores - top) * scale)
            total = jnp.sum(weights, axis=-1, keepdims=True)
            mixed = jnp.dot(weights.astype(BF16), all_values, preferred_element_type=F32)
            attended[start : start + rows, here] = (mixed / total).astype(BF16)
    width = own.shape[1]
    step = 512

    def one(block, carry):
        column = pl.ds(pl.multiple_of(block * step, step), step)
        weight = jnp.concatenate([own[:, column], other[:, column]], axis=0)
        result = jnp.dot(attended[...], weight, preferred_element_type=F32).astype(BF16)
        at = 0
        for out, size in zip(outs, cuts):
            out[:, column] = result[at : at + size]
            at += size
        return carry

    lax.fori_loop(0, width // step, one, 0)


def attend(queries, keys, values, far_keys, far_values, own, other, cuts):
    width = own.shape[1]
    return pl.pallas_call(
        functools.partial(attend_kernel, cuts),
        out_shape=[jax.ShapeDtypeStruct((size, width), BF16) for size in cuts],
        in_specs=[VMEM] * 7,
        out_specs=[VMEM] * len(cuts),
        scratch_shapes=[pltpu.VMEM((queries.shape[0], 2 * HDIM), BF16)],
        compiler_params=PARAMS,
    )(queries, keys, values, far_keys, far_values, own, other)


def gather_plane(part, first, second):
    near = jnp.concatenate(
        [part, send(part, first(1)), send(part, first(-1)), send(part, first(2))], axis=0
    )
    half = near.shape[0] // 2
    before, after = send(near, second(1)), send(near, second(-1))
    opposite_low = send(before[:half], second(1))
    opposite_high = send(after[half:], second(-1))
    return [near, before, after, opposite_low, opposite_high]


def scatter_plane(parts, first, second):
    near, before, after, opposite_low, opposite_high = parts
    half = near.shape[0] // 2
    low, high = send(opposite_low, second(1)), send(opposite_high, second(-1))
    to_after = jnp.concatenate(
        [(after[:half].astype(F32) + low.astype(F32)).astype(BF16), after[half:]], axis=0
    )
    to_before = jnp.concatenate(
        [before[:half], (before[half:].astype(F32) + high.astype(F32)).astype(BF16)], axis=0
    )
    from_before, from_after = send(to_after, second(1)), send(to_before, second(-1))
    total = near.astype(F32) + from_before.astype(F32) + from_after.astype(F32)
    size = near.shape[0] // 4
    kept, to_minus, to_plus, to_opposite = [total[i * size : (i + 1) * size] for i in range(4)]
    arrived = [
        send(to_plus.astype(BF16), first(1)),
        send(to_minus.astype(BF16), first(-1)),
        send(to_opposite.astype(BF16), first(2)),
    ]
    for value in arrived:
        kept = kept + value.astype(F32)
    return kept


def swap_weights(core, weight, axis):
    half = weight.shape[axis] // 2
    mine = send(lax.dynamic_slice_in_dim(weight, core * half, half, axis), to_both_sides)
    return mine, send(mine, to_other_core)


def on_device(
    trajectory, qkv_weight, out_weight, shift_table, scale_table, gate_table, step_sizes, window_start
):
    group = lax.axis_index("tm")
    core = group % 2
    index = window_start[0] + group
    state = trajectory[0]
    rows = state.shape[0]
    mine, theirs = swap_weights(core, qkv_weight, 1)
    out_mine, out_theirs = swap_weights(core, out_weight, 1)
    out_other = jnp.where(
        core == 0,
        jnp.concatenate([out_mine, out_theirs], axis=1),
        jnp.concatenate([out_theirs, out_mine], axis=1),
    )

    modulated = modulate(index[None], state, scale_table, shift_table)
    low = gather_plane(modulated[: rows // 2], along_x, along_z)
    high = gather_plane(modulated[rows // 2 :], along_z, along_x)
    pieces = low + high
    queries, keys, values = project(core[None], pieces, qkv_weight, mine, theirs)
    far_keys, far_values = send(keys, to_partner), send(values, to_partner)
    partial = attend(
        queries,
        keys,
        values,
        far_keys,
        far_values,
        out_weight,
        out_other,
        [piece.shape[0] for piece in pieces],
    )
    projected = jnp.concatenate(
        [
            scatter_plane(partial[:5], along_x, along_z),
            scatter_plane(partial[5:], along_z, along_x),
        ],
        axis=0,
    )
    gates = lax.dynamic_slice_in_dim(gate_table, index, 1, 0)
    step = lax.dynamic_slice_in_dim(step_sizes, index, 1, 0)[0]
    drift = step * (gates * projected)

    start = jnp.where(core == 0, state, send(state, to_later_core))
    start = jnp.where(group < 2, start, send(start, to_later_half))
    beside = send(drift.astype(BF16), to_other_core).astype(F32)
    earlier = send((drift + beside).astype(BF16), to_later_half).astype(F32)
    summed = drift + earlier + jnp.where(core == 1, beside, 0.0)
    return (start + summed)[None]


def solution(mesh):
    in_specs = (P("tm", "seq", None), P(None, None, "seq"), P("seq", None), P(), P(), P(), P(), P())
    out_specs = P("tm", "seq", None)
    return jax.shard_map(
        on_device, mesh=mesh, in_specs=in_specs, out_specs=out_specs, check_vma=False
    )
```

```python
import functools
import math

import jax
import jax.numpy as jnp
from jax import lax
from jax.experimental import pallas as pl
from jax.experimental.pallas import tpu as pltpu
from jax.sharding import PartitionSpec as P

HDIM = 128
XS, YLS, ZS = 4, 2, 4
BF16, F32 = jnp.bfloat16, jnp.float32
VMEM = pl.BlockSpec(memory_space=pltpu.VMEM)
SMEM = pl.BlockSpec(memory_space=pltpu.SMEM)
ANY = pl.BlockSpec(memory_space=pl.ANY)
PARAMS = pltpu.CompilerParams(vmem_limit_bytes=24 * 1024 * 1024)


def moves(rule):
    pairs = []
    for yh in range(2):
        for core in range(2):
            for x in range(XS):
                for yl in range(YLS):
                    for z in range(ZS):
                        to = rule(yh, core, x, yl, z)
                        if to is not None:
                            pairs.append((flat(yh, core, x, yl, z), flat(*to)))
    return pairs


def flat(yh, core, x, yl, z):
    return (((yh * 2 + core) * XS + x) * YLS + yl) * ZS + z


def send(value, rule):
    return lax.ppermute(value, ("tm", "seq"), moves(rule))


def first_axis(step):
    return lambda yh, core, x, yl, z: (
        (yh, core, (x + step) % XS, yl, z) if core == 0 else (yh, core, x, yl, (z + step) % ZS)
    )


def second_axis(step):
    return lambda yh, core, x, yl, z: (
        (yh, core, x, yl, (z + step) % ZS) if core == 0 else (yh, core, (x + step) % XS, yl, z)
    )


def to_other_core(yh, core, x, yl, z):
    return (yh, 1 - core, x, yl, z)


def to_partner(yh, core, x, yl, z):
    return (yh, core, x, 1 - yl, z)


def to_both_sides(yh, core, x, yl, z):
    return (yh if core == 0 else 1 - yh, core, x, 1 - yl, z)


def to_later_half(yh, core, x, yl, z):
    return (1, core, x, yl, z) if yh == 0 else None


def to_later_half_other_core(yh, core, x, yl, z):
    return (1, 1 - core, x, yl, z) if yh == 0 else None


def to_later_core(yh, core, x, yl, z):
    return (yh, 1, x, yl, z) if core == 0 else None


def modulate_kernel(index, state, scale, shift, out):
    row = index[0]
    value = state[...]
    mean = jnp.mean(value * value, axis=-1, keepdims=True)
    normed = value * lax.rsqrt(mean + 1e-06)
    out[...] = (normed * (1.0 + scale[pl.ds(row, 1), :]) + shift[pl.ds(row, 1), :]).astype(BF16)


def modulate(index, state, scale, shift):
    return pl.pallas_call(
        modulate_kernel,
        out_shape=jax.ShapeDtypeStruct(state.shape, BF16),
        in_specs=[SMEM, VMEM, VMEM, VMEM],
        out_specs=VMEM,
        compiler_params=PARAMS,
    )(index, state, scale, shift)


def project_kernel(count, chunk, *refs):
    core_ref, pieces, (own, mine, theirs), (queries, both_kv), total = (
        refs[0],
        refs[1 : 1 + count],
        refs[1 + count : 4 + count],
        refs[4 + count : 6 + count],
        refs[-1],
    )
    depth = own.shape[1]
    half = depth // 2
    wide = 2 * HDIM
    first = core_ref[0] * half
    total[...] = jnp.zeros_like(total)

    def side(weight, start):
        def one(step, carry):
            at = pl.multiple_of(step * chunk, chunk)
            column = pl.multiple_of(start + at, 128)
            rows = jnp.concatenate([piece[:, pl.ds(column, chunk)] for piece in pieces], axis=0)
            for kind in range(3):
                both = jnp.concatenate(
                    [own[kind, pl.ds(column, chunk), :], weight[kind, pl.ds(at, chunk), :]], axis=-1
                )
                total[kind] += jnp.dot(rows, both, preferred_element_type=F32)
            return carry

        lax.fori_loop(0, half // chunk, one, 0)

    side(mine, first)
    side(theirs, half - first)
    queries[...] = total[0].astype(BF16)
    both_kv[:, :wide] = total[1].astype(BF16)
    both_kv[:, wide:] = total[2].astype(BF16)


def project(core, pieces, own, mine, theirs):
    tokens = sum(piece.shape[0] for piece in pieces)
    wide = 2 * HDIM
    return pl.pallas_call(
        functools.partial(project_kernel, len(pieces), 512),
        out_shape=[
            jax.ShapeDtypeStruct((tokens, wide), BF16),
            jax.ShapeDtypeStruct((tokens, 2 * wide), BF16),
        ],
        in_specs=[SMEM] + [VMEM] * (len(pieces) + 3),
        out_specs=[VMEM] * 2,
        scratch_shapes=[pltpu.VMEM((3, tokens, wide), F32)],
        compiler_params=PARAMS,
    )(core, *pieces, own, mine, theirs)


def attend_kernel(count, cuts, core_ref, queries, own, mine, theirs, *refs):
    near, far, outs, attended = refs[:count], refs[count : 2 * count], refs[2 * count : -1], refs[-1]
    scale = 1.0 / math.sqrt(HDIM)
    contract = (((1,), (1,)), ((), ()))
    for head in range(2):
        here = slice(head * HDIM, (head + 1) * HDIM)
        there = slice((1 - head) * HDIM, (2 - head) * HDIM)
        here_v = slice((2 + head) * HDIM, (3 + head) * HDIM)
        there_v = slice((3 - head) * HDIM, (4 - head) * HDIM)
        all_keys = jnp.concatenate([r[:, here] for r in near] + [r[:, there] for r in far], axis=0)
        all_values = jnp.concatenate(
            [r[:, here_v] for r in near] + [r[:, there_v] for r in far], axis=0
        )
        scores = lax.dot_general(queries[:, here], all_keys, contract, preferred_element_type=F32)
        top = jnp.max(scores, axis=-1, keepdims=True)
        weights = jnp.exp((scores - top) * scale)
        total = jnp.sum(weights, axis=-1, keepdims=True)
        mixed = jnp.dot(weights.astype(BF16), all_values, preferred_element_type=F32)
        attended[:, here] = (mixed / total).astype(BF16)
    half = own.shape[1] // 2
    step = 512
    first = core_ref[0] * half

    def side(weight, start):
        def one(block, carry):
            at = pl.multiple_of(block * step, step)
            column = pl.ds(pl.multiple_of(start + at, 128), step)
            both = jnp.concatenate([own[:, column], weight[:, pl.ds(at, step)]], axis=0)
            result = jnp.dot(attended[...], both, preferred_element_type=F32).astype(BF16)
            row = 0
            for out, size in zip(outs, cuts):
                out[:, column] = result[row : row + size]
                row += size
            return carry

        lax.fori_loop(0, half // step, one, 0)

    side(mine, first)
    side(theirs, half - first)


def attend(core, queries, near, far, own, mine, theirs, cuts):
    width = own.shape[1]
    return pl.pallas_call(
        functools.partial(attend_kernel, len(near), cuts),
        out_shape=[jax.ShapeDtypeStruct((size, width), BF16) for size in cuts],
        in_specs=[SMEM] + [VMEM] * (4 + 2 * len(near)),
        out_specs=[VMEM] * len(cuts),
        scratch_shapes=[pltpu.VMEM((queries.shape[0], 2 * HDIM), BF16)],
        compiler_params=PARAMS,
    )(core, queries, own, mine, theirs, *near, *far)


def join_kernel(before, after, low, high, unused, to_before, to_after):
    half = low.shape[0]
    to_after[:half] = (after[:half].astype(F32) + low[...].astype(F32)).astype(BF16)
    to_after[half:] = after[half:]
    to_before[:half] = before[:half]
    to_before[half:] = (before[half:].astype(F32) + high[...].astype(F32)).astype(BF16)


def join(before, after, low, high, start):
    return pl.pallas_call(
        join_kernel,
        out_shape=[jax.ShapeDtypeStruct(before.shape, BF16)] * 2,
        in_specs=[VMEM] * 4 + [ANY],
        out_specs=[VMEM] * 2,
        compiler_params=PARAMS,
    )(before, after, low, high, start)


def split_kernel(near, one, two, kept, *outs):
    size = kept.shape[0]
    for place in range(4):
        rows = slice(place * size, (place + 1) * size)
        total = near[rows].astype(F32) + one[rows].astype(F32) + two[rows].astype(F32)
        if place == 0:
            kept[...] = total
        else:
            outs[place - 1][...] = total.astype(BF16)


def split(near, one, two):
    size, width = near.shape[0] // 4, near.shape[1]
    return pl.pallas_call(
        split_kernel,
        out_shape=[jax.ShapeDtypeStruct((size, width), F32)]
        + [jax.ShapeDtypeStruct((size, width), BF16)] * 3,
        in_specs=[VMEM] * 3,
        out_specs=[VMEM] * 4,
        compiler_params=PARAMS,
    )(near, one, two)


def swap_weights(core, weight, axis):
    half = weight.shape[axis] // 2
    mine = send(lax.dynamic_slice_in_dim(weight, core * half, half, axis), to_both_sides)
    return mine, send(mine, to_other_core)


def on_device(
    trajectory, qkv_weight, out_weight, shift_table, scale_table, gate_table, step_sizes, window_start
):
    group = lax.axis_index("tm")
    core = group % 2
    index = window_start[0] + group
    state = trajectory[0]
    rows = state.shape[0]
    mine, theirs = swap_weights(core, qkv_weight, 1)
    out_mine, out_theirs = swap_weights(core, out_weight, 1)

    modulated = modulate(index[None], state, scale_table, shift_table)
    near = jnp.concatenate([modulated] + [send(modulated, first_axis(s)) for s in (1, -1, 2)], axis=0)
    half = near.shape[0] // 2
    before, after = send(near, second_axis(1)), send(near, second_axis(-1))
    low, high = send(before[:half], second_axis(1)), send(after[half:], second_axis(-1))

    place = core[None]
    weights = (qkv_weight, mine, theirs)
    near_q, near_kv = project(place, [near], *weights)
    side_q, side_kv = project(place, [before, after], *weights)
    last_q, last_kv = project(place, [low, high], *weights)
    kv = [near_kv, side_kv, last_kv]
    far = [send(value, to_partner) for value in kv]

    start = jnp.where(core == 0, state, send(state, to_later_core))
    start = jnp.where(group < 2, start, send(start, to_later_half))

    outs = (out_weight, out_mine, out_theirs)
    size = near.shape[0]
    last_low, last_high = attend(place, last_q, kv, far, *outs, [half, half])
    side_before, side_after = attend(place, side_q, kv, far, *outs, [size, size])
    (kept,) = attend(place, near_q, kv, far, *outs, [size])

    from_low, from_high = send(last_low, second_axis(1)), send(last_high, second_axis(-1))
    to_before, to_after = join(side_before, side_after, from_low, from_high, start)
    from_before, from_after = send(to_after, second_axis(1)), send(to_before, second_axis(-1))
    total, to_minus, to_plus, to_opposite = split(kept, from_before, from_after)
    for value, s in ((to_plus, 1), (to_minus, -1), (to_opposite, 2)):
        total = total + send(value, first_axis(s)).astype(F32)

    gates = lax.dynamic_slice_in_dim(gate_table, index, 1, 0)
    step = lax.dynamic_slice_in_dim(step_sizes, index, 1, 0)[0]
    drift = step * (gates * total)
    term = drift.astype(BF16)
    summed = drift
    for rule in (to_later_half, to_later_half_other_core, to_later_core):
        summed = summed + send(term, rule).astype(F32)
    return (start + summed)[None]


def solution(mesh):
    in_specs = (P("tm", "seq", None), P(None, None, "seq"), P("seq", None), P(), P(), P(), P(), P())
    out_specs = P("tm", "seq", None)
    return jax.shard_map(
        on_device, mesh=mesh, in_specs=in_specs, out_specs=out_specs, check_vma=False
    )
```

```python
import functools
import math

import jax
import jax.numpy as jnp
from jax import lax
from jax.experimental import pallas as pl
from jax.experimental.pallas import tpu as pltpu
from jax.sharding import PartitionSpec as P

HDIM = 128
XS, YLS, ZS = 4, 2, 4
BF16, F32 = jnp.bfloat16, jnp.float32
VMEM = pl.BlockSpec(memory_space=pltpu.VMEM)
SMEM = pl.BlockSpec(memory_space=pltpu.SMEM)
ANY = pl.BlockSpec(memory_space=pl.ANY)
PARAMS = pltpu.CompilerParams(vmem_limit_bytes=24 * 1024 * 1024)


def moves(rule):
    pairs = []
    for yh in range(2):
        for core in range(2):
            for x in range(XS):
                for yl in range(YLS):
                    for z in range(ZS):
                        to = rule(yh, core, x, yl, z)
                        if to is not None:
                            pairs.append((flat(yh, core, x, yl, z), flat(*to)))
    return pairs


def flat(yh, core, x, yl, z):
    return (((yh * 2 + core) * XS + x) * YLS + yl) * ZS + z


def send(value, rule):
    return lax.ppermute(value, ("tm", "seq"), moves(rule))


def first_axis(step):
    return lambda yh, core, x, yl, z: (
        (yh, core, (x + step) % XS, yl, z) if core == 0 else (yh, core, x, yl, (z + step) % ZS)
    )


def second_axis(step):
    return lambda yh, core, x, yl, z: (
        (yh, core, x, yl, (z + step) % ZS) if core == 0 else (yh, core, (x + step) % XS, yl, z)
    )


def to_other_core(yh, core, x, yl, z):
    return (yh, 1 - core, x, yl, z)


def to_partner(yh, core, x, yl, z):
    return (yh, core, x, 1 - yl, z)


def to_both_sides(yh, core, x, yl, z):
    return (yh if core == 0 else 1 - yh, core, x, 1 - yl, z)


def to_later_half(yh, core, x, yl, z):
    return (1, core, x, yl, z) if yh == 0 else None


def to_later_half_other_core(yh, core, x, yl, z):
    return (1, 1 - core, x, yl, z) if yh == 0 else None


def to_later_core(yh, core, x, yl, z):
    return (yh, 1, x, yl, z) if core == 0 else None


def modulate_kernel(index, state, scale, shift, out):
    row = lax.rem(index[0], 8)
    value = state[...]
    mean = jnp.mean(value * value, axis=-1, keepdims=True)
    normed = value * lax.rsqrt(mean + 1e-06)
    out[...] = (normed * (1.0 + scale[pl.ds(row, 1), :]) + shift[pl.ds(row, 1), :]).astype(BF16)


def modulate(index, state, scale, shift):
    rows, width = state.shape
    table = pl.BlockSpec((8, width), lambda i, index: (lax.div(index[0], 8), 0))
    whole = pl.BlockSpec((rows, width), lambda i, index: (0, 0))
    return pl.pallas_call(
        modulate_kernel,
        grid_spec=pltpu.PrefetchScalarGridSpec(
            num_scalar_prefetch=1, grid=(1,), in_specs=[whole, table, table], out_specs=whole
        ),
        out_shape=jax.ShapeDtypeStruct(state.shape, BF16),
        compiler_params=PARAMS,
        cost_estimate=pl.CostEstimate(flops=1000000, bytes_accessed=2000000, transcendentals=0),
    )(index, state, scale, shift)


def halves(block, steps):
    return (
        lambda k, core: lax.rem(k + core[0] * steps, 2 * steps),
        lambda k, core: jnp.minimum(k, steps - 1),
        lambda k, core: jnp.maximum(k - steps, 0),
    )


def project_kernel(count, kinds, steps, rows, core, *refs):
    pieces, own = refs[:count], refs[count : count + kinds]
    mine, theirs = refs[count + kinds : count + kinds + 2]
    outs, total = refs[count + kinds + 2 : -1], refs[-1]
    k = pl.program_id(0)
    left = jnp.concatenate([piece[...] for piece in pieces], axis=0)

    def add(other):
        for kind in range(kinds):
            both = jnp.concatenate([own[kind][0], other[kind]], axis=-1)
            part = jnp.dot(left, both, preferred_element_type=F32)

            @pl.when(k == 0)
            def _():
                total[kind] = part

            @pl.when(k > 0)
            def _():
                total[kind] += part

    pl.when(k < steps)(lambda: add(mine))
    pl.when(k >= steps)(lambda: add(theirs))

    @pl.when(k == 2 * steps - 1)
    def _():
        at = 0
        for out, size in zip(outs, rows):
            for kind in range(kinds):
                out[:, kind * 2 * HDIM : (kind + 1) * 2 * HDIM] = total[
                    kind, at : at + size
                ].astype(BF16)
            at += size


def project(core, pieces, weight, kinds, mine, theirs, rows):
    tokens = sum(rows)
    wide = 2 * HDIM
    depth = weight.shape[1]
    steps = 2
    block = depth // (2 * steps)
    place, near, later = halves(block, steps)
    in_specs = [
        pl.BlockSpec((piece.shape[0], block), lambda k, core: (0, place(k, core)))
        for piece in pieces
    ]
    in_specs += [
        pl.BlockSpec((1, block, HDIM), lambda k, core, kind=kind: (kind, place(k, core), 0))
        for kind in kinds
    ]
    in_specs += [
        pl.BlockSpec((len(kinds), block, HDIM), lambda k, core, at=at: (0, at(k, core), 0))
        for at in (near, later)
    ]
    return pl.pallas_call(
        functools.partial(project_kernel, len(pieces), len(kinds), steps, rows),
        grid_spec=pltpu.PrefetchScalarGridSpec(
            num_scalar_prefetch=1,
            grid=(2 * steps,),
            in_specs=in_specs,
            out_specs=[
                pl.BlockSpec((size, len(kinds) * wide), lambda k, core: (0, 0)) for size in rows
            ],
            scratch_shapes=[pltpu.VMEM((len(kinds), tokens, wide), F32)],
        ),
        out_shape=[jax.ShapeDtypeStruct((size, len(kinds) * wide), BF16) for size in rows],
        compiler_params=PARAMS,
        cost_estimate=pl.CostEstimate(
            flops=2 * tokens * depth * wide * len(kinds), bytes_accessed=10000000, transcendentals=0
        ),
    )(core, *pieces, *[weight] * len(kinds), mine, theirs)


def attend_kernel(count, steps, cuts, core, queries, *refs):
    near, far, refs = refs[:count], refs[count : 2 * count], refs[2 * count :]
    own, mine, theirs, outs, attended = refs[0], refs[1], refs[2], refs[-1 - len(cuts) : -1], refs[-1]
    k = pl.program_id(0)

    @pl.when(k == 0)
    def _():
        scale = 1.0 / math.sqrt(HDIM)
        contract = (((1,), (1,)), ((), ()))
        for head in range(2):
            here = slice(head * HDIM, (head + 1) * HDIM)
            there = slice((1 - head) * HDIM, (2 - head) * HDIM)
            here_v = slice((2 + head) * HDIM, (3 + head) * HDIM)
            there_v = slice((3 - head) * HDIM, (4 - head) * HDIM)
            all_keys = jnp.concatenate(
                [r[:, here] for r in near] + [r[:, there] for r in far], axis=0
            )
            all_values = jnp.concatenate(
                [r[:, here_v] for r in near] + [r[:, there_v] for r in far], axis=0
            )
            scores = lax.dot_general(
                queries[:, here], all_keys, contract, preferred_element_type=F32
            )
            top = jnp.max(scores, axis=-1, keepdims=True)
            weights = jnp.exp((scores - top) * scale)
            total = jnp.sum(weights, axis=-1, keepdims=True)
            mixed = jnp.dot(weights.astype(BF16), all_values, preferred_element_type=F32)
            attended[:, here] = (mixed / total).astype(BF16)

    def out(other):
        both = jnp.concatenate([own[...], other[...]], axis=0)
        result = jnp.dot(attended[...], both, preferred_element_type=F32).astype(BF16)
        row = 0
        for out, size in zip(outs, cuts):
            out[...] = result[row : row + size]
            row += size

    pl.when(k < steps)(lambda: out(mine))
    pl.when(k >= steps)(lambda: out(theirs))


def attend(core, queries, near, far, own, mine, theirs, cuts, passed=None):
    width = own.shape[1]
    tokens = queries.shape[0]
    steps = 2
    block = width // (2 * steps)
    place, first, later = halves(block, steps)
    in_specs = [
        pl.BlockSpec(value.shape, lambda k, core: (0, 0)) for value in (queries, *near, *far)
    ]
    in_specs += [
        pl.BlockSpec((HDIM, block), lambda k, core, at=at: (0, at(k, core)))
        for at in (place, first, later)
    ]
    out_specs = [pl.BlockSpec((size, block), lambda k, core: (0, place(k, core))) for size in cuts]
    out_shape = [jax.ShapeDtypeStruct((size, width), BF16) for size in cuts]
    extra, aliases = [], {}
    if passed is not None:
        aliases = {1 + len(in_specs): 0}
        in_specs, out_specs = in_specs + [ANY], [ANY] + out_specs
        out_shape = [jax.ShapeDtypeStruct(passed.shape, passed.dtype)] + out_shape
        extra = [passed]
    return pl.pallas_call(
        functools.partial(attend_kernel, len(near), steps, cuts),
        grid_spec=pltpu.PrefetchScalarGridSpec(
            num_scalar_prefetch=1,
            grid=(2 * steps,),
            in_specs=in_specs,
            out_specs=out_specs,
            scratch_shapes=[pltpu.VMEM((tokens, 2 * HDIM), BF16)],
        ),
        out_shape=out_shape,
        input_output_aliases=aliases,
        compiler_params=PARAMS,
        cost_estimate=pl.CostEstimate(
            flops=4 * tokens * HDIM * (width + 2048), bytes_accessed=8000000, transcendentals=0
        ),
    )(core, queries, *near, *far, own, mine, theirs, *extra)


def join_kernel(after, before, low, high, to_after, to_before):
    to_after[...] = (after[...].astype(F32) + low[...].astype(F32)).astype(BF16)
    to_before[...] = (before[...].astype(F32) + high[...].astype(F32)).astype(BF16)


def join(after, before, low, high):
    return pl.pallas_call(
        join_kernel,
        out_shape=[jax.ShapeDtypeStruct(before.shape, BF16)] * 2,
        in_specs=[VMEM] * 4,
        out_specs=[VMEM] * 2,
        compiler_params=PARAMS,
    )(after, before, low, high)


def split_kernel(near_low, near_high, low_1, low_2, high_1, high_2, kept, to_minus, to_plus, to_opposite):
    size = kept.shape[0]

    def total(near, one, two, rows):
        return near[rows].astype(F32) + one[rows].astype(F32) + two[rows].astype(F32)

    kept[...] = total(near_low, low_1, low_2, slice(0, size))
    to_minus[...] = total(near_low, low_1, low_2, slice(size, 2 * size)).astype(BF16)
    to_plus[...] = total(near_high, high_1, high_2, slice(0, size)).astype(BF16)
    to_opposite[...] = total(near_high, high_1, high_2, slice(size, 2 * size)).astype(BF16)


def split(*parts):
    size, width = parts[0].shape[0] // 2, parts[0].shape[1]
    return pl.pallas_call(
        split_kernel,
        out_shape=[jax.ShapeDtypeStruct((size, width), F32)]
        + [jax.ShapeDtypeStruct((size, width), BF16)] * 3,
        in_specs=[VMEM] * 6,
        out_specs=[VMEM] * 4,
        compiler_params=PARAMS,
    )(*parts)


def swap_weights(core, weight, axis):
    half = weight.shape[axis] // 2
    mine = send(lax.dynamic_slice_in_dim(weight, core * half, half, axis), to_both_sides)
    return mine, send(mine, to_other_core)


def on_device(
    trajectory, qkv_weight, out_weight, shift_table, scale_table, gate_table, step_sizes, window_start
):
    group = lax.axis_index("tm")
    core = group % 2
    index = window_start[0] + group
    state = trajectory[0]
    rows = state.shape[0]
    kv_mine, kv_theirs = swap_weights(core, qkv_weight[1:], 1)
    q_mine, q_theirs = swap_weights(core, qkv_weight[:1], 1)
    out_mine, out_theirs = swap_weights(core, out_weight, 1)

    modulated = modulate(index[None], state, scale_table, shift_table)
    minus, plus, opposite = [send(modulated, first_axis(s)) for s in (1, -1, 2)]
    near_low = jnp.concatenate([modulated, minus], axis=0)
    before_low, after_low = send(near_low, second_axis(1)), send(near_low, second_axis(-1))
    near_high = jnp.concatenate([plus, opposite], axis=0)
    after_high, before_high = send(near_high, second_axis(-1)), send(near_high, second_axis(1))
    last_low, last_high = send(before_low, second_axis(1)), send(after_high, second_axis(-1))

    place = core[None]
    size = near_low.shape[0]
    near = [near_low, near_high]
    side = [before_low, before_high, after_low, after_high]
    last = [last_low, last_high]
    kv = [
        project(place, pieces, qkv_weight, (1, 2), kv_mine, kv_theirs, [size * len(pieces)])[0]
        for pieces in (near, side, last)
    ]
    far = [send(value, to_partner) for value in kv]
    near_q, side_q, last_q = project(
        place,
        near + side + last,
        qkv_weight,
        (0,),
        q_mine,
        q_theirs,
        [2 * size, 4 * size, 2 * size],
    )

    start = jnp.where(core == 0, state, send(state, to_later_core))

    outs = (out_weight, out_mine, out_theirs)
    start, last_low, last_high = attend(place, last_q, kv, far, *outs, [size] * 2, start)
    from_low, from_high = send(last_low, second_axis(1)), send(last_high, second_axis(-1))
    start = jnp.where(group < 2, start, send(start, to_later_half))
    before_low, before_high, after_low, after_high = attend(
        place, side_q, kv, far, *outs, [size] * 4
    )
    high_1, low_2 = send(after_high, second_axis(1)), send(before_low, second_axis(-1))
    near_low, near_high = attend(place, near_q, kv, far, *outs, [size] * 2)
    after_low, before_high = join(after_low, before_high, from_low, from_high)
    low_1, high_2 = send(after_low, second_axis(1)), send(before_high, second_axis(-1))
    total, to_minus, to_plus, to_opposite = split(near_low, near_high, low_1, low_2, high_1, high_2)
    for value, s in ((to_plus, 1), (to_minus, -1), (to_opposite, 2)):
        total = total + send(value, first_axis(s)).astype(F32)

    gates = lax.dynamic_slice_in_dim(gate_table, index, 1, 0)
    step = lax.dynamic_slice_in_dim(step_sizes, index, 1, 0)[0]
    drift = step * (gates * total)
    term = drift.astype(BF16)
    summed = drift
    for rule in (to_later_half, to_later_half_other_core, to_later_core):
        summed = summed + send(term, rule).astype(F32)
    return (start + summed)[None]


def solution(mesh):
    in_specs = (P("tm", "seq", None), P(None, None, "seq"), P("seq", None), P(), P(), P(), P(), P())
    out_specs = P("tm", "seq", None)
    return jax.shard_map(
        on_device, mesh=mesh, in_specs=in_specs, out_specs=out_specs, check_vma=False
    )
```

```python
import functools
import math

import jax
import jax.numpy as jnp
from jax import lax
from jax.experimental import pallas as pl
from jax.experimental.pallas import tpu as pltpu
from jax.sharding import PartitionSpec as P

HDIM = 128
XS, YLS, ZS = 4, 2, 4
BF16, F32 = jnp.bfloat16, jnp.float32
VMEM = pl.BlockSpec(memory_space=pltpu.VMEM)
SMEM = pl.BlockSpec(memory_space=pltpu.SMEM)
ANY = pl.BlockSpec(memory_space=pl.ANY)
PARAMS = pltpu.CompilerParams(vmem_limit_bytes=20 * 1024 * 1024)
WIDE = pltpu.CompilerParams(vmem_limit_bytes=60 * 1024 * 1024)


def moves(rule):
    pairs = []
    for yh in range(2):
        for core in range(2):
            for x in range(XS):
                for yl in range(YLS):
                    for z in range(ZS):
                        to = rule(yh, core, x, yl, z)
                        if to is not None:
                            pairs.append((flat(yh, core, x, yl, z), flat(*to)))
    return pairs


def flat(yh, core, x, yl, z):
    return (((yh * 2 + core) * XS + x) * YLS + yl) * ZS + z


def send(value, rule):
    return lax.ppermute(value, ("tm", "seq"), moves(rule))


def first_axis(step):
    return lambda yh, core, x, yl, z: (
        (yh, core, (x + step) % XS, yl, z) if core == 0 else (yh, core, x, yl, (z + step) % ZS)
    )


def second_axis(step):
    return lambda yh, core, x, yl, z: (
        (yh, core, x, yl, (z + step) % ZS) if core == 0 else (yh, core, (x + step) % XS, yl, z)
    )


def to_other_core(yh, core, x, yl, z):
    return (yh, 1 - core, x, yl, z)


def to_partner(yh, core, x, yl, z):
    return (yh, core, x, 1 - yl, z)


def to_both_sides(yh, core, x, yl, z):
    return (yh if core == 0 else 1 - yh, core, x, 1 - yl, z)


def to_later_half(yh, core, x, yl, z):
    return (1, core, x, yl, z) if yh == 0 else None


def from_first(yh_to, core_to):
    return lambda yh, core, x, yl, z: (yh_to, core_to, x, yl, z) if yh == 0 and core == 0 else None


def modulate_kernel(index, state, scale, shift, gate, out, gates):
    row = pl.ds(lax.rem(index[0], 8), 1)
    value = state[...]
    mean = jnp.mean(value * value, axis=-1, keepdims=True)
    normed = value * lax.rsqrt(mean + 1e-06)
    out[...] = (normed * (1.0 + scale[row, :]) + shift[row, :]).astype(BF16)
    gates[...] = gate[row, :]


def modulate(index, state, scale, shift, gate):
    rows, width = state.shape
    table = pl.BlockSpec((8, width), lambda i, index: (lax.div(index[0], 8), 0))
    whole = pl.BlockSpec((rows, width), lambda i, index: (0, 0))
    return pl.pallas_call(
        modulate_kernel,
        grid_spec=pltpu.PrefetchScalarGridSpec(
            num_scalar_prefetch=1,
            grid=(1,),
            in_specs=[whole, table, table, table],
            out_specs=[whole, pl.BlockSpec((1, width), lambda i, index: (0, 0))],
        ),
        out_shape=[
            jax.ShapeDtypeStruct(state.shape, BF16),
            jax.ShapeDtypeStruct((1, width), F32),
        ],
        compiler_params=WIDE,
        cost_estimate=pl.CostEstimate(flops=1000000, bytes_accessed=2000000, transcendentals=0),
    )(index, state, scale, shift, gate)


def pack_kernel(core, qkv, out, half):
    del core
    half[:3] = qkv[...]
    for block in range(out.shape[1] // HDIM):
        here = slice(block * HDIM, (block + 1) * HDIM)
        half[3, here, :] = out[:, here]


def pack(core, qkv_weight, out_weight):
    half = qkv_weight.shape[1] // 2
    return pl.pallas_call(
        pack_kernel,
        grid_spec=pltpu.PrefetchScalarGridSpec(
            num_scalar_prefetch=1,
            grid=(1,),
            in_specs=[
                pl.BlockSpec((3, half, HDIM), lambda i, core: (0, core[0], 0)),
                pl.BlockSpec((HDIM, half), lambda i, core: (0, core[0])),
            ],
            out_specs=pl.BlockSpec((4, half, HDIM), lambda i, core: (0, 0, 0)),
        ),
        out_shape=jax.ShapeDtypeStruct((4, half, HDIM), BF16),
        compiler_params=WIDE,
        cost_estimate=pl.CostEstimate(flops=0, bytes_accessed=4000000, transcendentals=0),
    )(core, qkv_weight, out_weight)


def stack_kernel(one, two, out):
    size = one.shape[0]
    out[:size] = one[...]
    out[size:] = two[...]


def stack(one, two):
    return pl.pallas_call(
        stack_kernel,
        out_shape=jax.ShapeDtypeStruct((2 * one.shape[0], one.shape[1]), one.dtype),
        in_specs=[VMEM] * 2,
        out_specs=VMEM,
        compiler_params=PARAMS,
    )(one, two)


def sides(core, mine, theirs, width, step, one):
    half = width // 2
    first = core[0] * half

    def side(weight, start):
        def body(block, carry):
            at = pl.multiple_of(block * step, step)
            one(weight, at, pl.multiple_of(start + at, 128))
            return carry

        lax.fori_loop(0, half // step, body, 0, unroll=True)

    side(mine, first)
    side(theirs, half - first)


def project_kernel(count, rows, core, *refs):
    pieces, (own, mine, theirs) = refs[:count], refs[count : count + 3]
    both_kv, queries, total = refs[count + 3], refs[count + 4 : -1], refs[-1]
    step, wide = 512, 2 * HDIM
    total[...] = jnp.zeros_like(total)

    def one(weight, at, column):
        left = jnp.concatenate([piece[:, pl.ds(column, step)] for piece in pieces], axis=0)
        for kind in range(3):
            both = jnp.concatenate(
                [own[kind, pl.ds(column, step), :], weight[kind, pl.ds(at, step), :]], axis=-1
            )
            total[kind] += jnp.dot(left, both, preferred_element_type=F32)

    sides(core, mine, theirs, own.shape[1], step, one)
    both_kv[:, :wide] = total[1].astype(BF16)
    both_kv[:, wide:] = total[2].astype(BF16)
    at = 0
    for out, size in zip(queries, rows):
        out[...] = total[0, at : at + size].astype(BF16)
        at += size


def project(core, pieces, weight, mine, theirs, rows):
    wide = 2 * HDIM
    tokens, depth = sum(rows), weight.shape[1]
    return pl.pallas_call(
        functools.partial(project_kernel, len(pieces), rows),
        out_shape=[jax.ShapeDtypeStruct((tokens, 2 * wide), BF16)]
        + [jax.ShapeDtypeStruct((size, wide), BF16) for size in rows],
        in_specs=[SMEM] + [VMEM] * (len(pieces) + 3),
        out_specs=[VMEM] * (1 + len(rows)),
        scratch_shapes=[pltpu.VMEM((3, tokens, wide), F32)],
        compiler_params=PARAMS,
        cost_estimate=pl.CostEstimate(
            flops=6 * tokens * depth * wide, bytes_accessed=1000000, transcendentals=0
        ),
    )(core, *pieces, weight, mine, theirs)


def attend_kernel(count, cuts, core, queries, own, mine, theirs, *refs):
    near, far = refs[:count], refs[count : 2 * count]
    outs, attended = refs[2 * count : -1], refs[-1]
    scale = 1.0 / math.sqrt(HDIM)
    contract = (((1,), (1,)), ((), ()))
    for head in range(2):
        here = slice(head * HDIM, (head + 1) * HDIM)
        there = slice((1 - head) * HDIM, (2 - head) * HDIM)
        here_v = slice((2 + head) * HDIM, (3 + head) * HDIM)
        there_v = slice((3 - head) * HDIM, (4 - head) * HDIM)
        all_keys = jnp.concatenate([r[:, here] for r in near] + [r[:, there] for r in far], axis=0)
        all_values = jnp.concatenate(
            [r[:, here_v] for r in near] + [r[:, there_v] for r in far], axis=0
        )
        scores = lax.dot_general(queries[:, here], all_keys, contract, preferred_element_type=F32)
        top = jnp.max(scores, axis=-1, keepdims=True)
        weights = jnp.exp((scores - top) * scale)
        total = jnp.sum(weights, axis=-1, keepdims=True)
        mixed = jnp.dot(weights.astype(BF16), all_values, preferred_element_type=F32)
        attended[:, here] = (mixed / total).astype(BF16)
    step = 512

    def one(weight, at, column):
        blocks = [
            weight[3, pl.ds(pl.multiple_of(at + i, HDIM), HDIM), :] for i in range(0, step, HDIM)
        ]
        both = jnp.concatenate(
            [own[:, pl.ds(column, step)], jnp.concatenate(blocks, axis=1)], axis=0
        )
        result = jnp.dot(attended[...], both, preferred_element_type=F32).astype(BF16)
        row = 0
        for out, size in zip(outs, cuts):
            out[:, pl.ds(column, step)] = result[row : row + size]
            row += size

    sides(core, mine, theirs, own.shape[1], step, one)


def attend(core, queries, near, far, own, mine, theirs, cuts):
    width = own.shape[1]
    tokens = queries.shape[0]
    return pl.pallas_call(
        functools.partial(attend_kernel, len(near), cuts),
        out_shape=[jax.ShapeDtypeStruct((size, width), BF16) for size in cuts],
        in_specs=[SMEM] + [VMEM] * (4 + 2 * len(near)),
        out_specs=[VMEM] * len(cuts),
        scratch_shapes=[pltpu.VMEM((tokens, 2 * HDIM), BF16)],
        compiler_params=PARAMS,
        cost_estimate=pl.CostEstimate(
            flops=4 * tokens * HDIM * (width + 2048), bytes_accessed=1000000, transcendentals=0
        ),
    )(core, queries, own, mine, theirs, *near, *far)


def join_kernel(after, before, low, high, to_after, to_before):
    to_after[...] = (after[...].astype(F32) + low[...].astype(F32)).astype(BF16)
    to_before[...] = (before[...].astype(F32) + high[...].astype(F32)).astype(BF16)


def join(after, before, low, high):
    return pl.pallas_call(
        join_kernel,
        out_shape=[jax.ShapeDtypeStruct(before.shape, BF16)] * 2,
        in_specs=[VMEM] * 4,
        out_specs=[VMEM] * 2,
        compiler_params=PARAMS,
    )(after, before, low, high)


def split_kernel(*refs):
    near_low, near_high, low_1, low_2, high_1, high_2 = refs[:6]
    kept, to_minus, to_plus, to_opposite = refs[-4:]
    size = kept.shape[0]

    def total(near, one, two, rows):
        return near[rows].astype(F32) + one[rows].astype(F32) + two[rows].astype(F32)

    kept[...] = total(near_low, low_1, low_2, slice(0, size))
    to_minus[...] = total(near_low, low_1, low_2, slice(size, 2 * size)).astype(BF16)
    to_plus[...] = total(near_high, high_1, high_2, slice(0, size)).astype(BF16)
    to_opposite[...] = total(near_high, high_1, high_2, slice(size, 2 * size)).astype(BF16)


def split(parts, until):
    size, width = parts[0].shape[0] // 2, parts[0].shape[1]
    return pl.pallas_call(
        split_kernel,
        out_shape=[jax.ShapeDtypeStruct((size, width), F32)]
        + [jax.ShapeDtypeStruct((size, width), BF16)] * 3,
        in_specs=[VMEM] * 6 + [ANY] * len(until),
        out_specs=[VMEM] * 4,
        compiler_params=PARAMS,
    )(*parts, *until)


def drift_kernel(index, steps, total, one, two, three, gates, drift, term):
    moved = total[...] + one[...].astype(F32) + two[...].astype(F32) + three[...].astype(F32)
    result = steps[index[0]] * (gates[...] * moved)
    drift[...] = result
    term[...] = result.astype(BF16)


def drifts(index, steps, total, arrived, gates):
    return pl.pallas_call(
        drift_kernel,
        out_shape=[
            jax.ShapeDtypeStruct(total.shape, F32),
            jax.ShapeDtypeStruct(total.shape, BF16),
        ],
        in_specs=[SMEM] * 2 + [VMEM] * 5,
        out_specs=[VMEM] * 2,
        compiler_params=PARAMS,
    )(index, steps, total, *arrived, gates)


def both_kernel(drift, beside, term):
    term[...] = (drift[...] + beside[...].astype(F32)).astype(BF16)


def both_cores(drift, beside):
    return pl.pallas_call(
        both_kernel,
        out_shape=jax.ShapeDtypeStruct(drift.shape, BF16),
        in_specs=[VMEM] * 2,
        out_specs=VMEM,
        compiler_params=PARAMS,
    )(drift, beside)


def finish_kernel(place, start, one, two, three, drift, beside, earlier, out):
    first = jnp.where(place[0] == 0, start[...], one[...] + two[...] + three[...])
    on_second = jnp.where(lax.rem(place[0], 2) == 1, beside[...].astype(F32), 0.0)
    out[...] = first + (drift[...] + on_second + earlier[...].astype(F32))


def finish(place, *parts):
    return pl.pallas_call(
        finish_kernel,
        out_shape=jax.ShapeDtypeStruct(parts[0].shape, F32),
        in_specs=[SMEM] + [VMEM] * 7,
        out_specs=VMEM,
        compiler_params=PARAMS,
    )(place, *parts)


def hold_kernel(value, *refs):
    del value, refs


def hold(value, *until):
    return pl.pallas_call(
        hold_kernel,
        out_shape=jax.ShapeDtypeStruct(value.shape, value.dtype),
        in_specs=[ANY] * (1 + len(until)),
        out_specs=ANY,
        input_output_aliases={0: 0},
        compiler_params=PARAMS,
    )(value, *until)


def on_device(
    trajectory, qkv_weight, out_weight, shift_table, scale_table, gate_table, step_sizes, window_start
):
    group = lax.axis_index("tm")
    core = group & 1
    place, core, index = group[None], core[None], window_start + group
    state = trajectory[0]
    mine = send(pack(core, qkv_weight, out_weight), to_both_sides)
    modulated, gates = modulate(index, state, scale_table, shift_table, gate_table)
    minus, plus, opposite = [send(modulated, first_axis(s)) for s in (1, -1, 2)]
    near_low = stack(modulated, minus)
    before_low, after_low = send(near_low, second_axis(1)), send(near_low, second_axis(-1))
    near_high = stack(plus, opposite)
    after_high, before_high = send(near_high, second_axis(-1)), send(near_high, second_axis(1))
    last_low, last_high = send(before_low, second_axis(1)), send(after_high, second_axis(-1))

    size = near_low.shape[0]
    near = [near_low, near_high]
    side = [before_low, before_high, after_low, after_high]
    last = [last_low, last_high]
    mine = hold(mine, *side)
    weights = (qkv_weight, mine, send(mine, to_other_core))
    first_kv, near_q, side_q = project(core, near + side, *weights, [2 * size, 4 * size])
    last_kv, last_q = project(core, last, *weights, [2 * size])
    kv = [first_kv, last_kv]
    far = [send(value, to_partner) for value in kv]

    outs = (out_weight, *weights[1:])
    last_low, last_high = attend(core, last_q, kv, far, *outs, [size] * 2)
    from_low, from_high = send(last_low, second_axis(1)), send(last_high, second_axis(-1))
    before_low, before_high, after_low, after_high = attend(
        core, side_q, kv, far, *outs, [size] * 4
    )
    high_1, low_2 = send(after_high, second_axis(1)), send(before_low, second_axis(-1))
    near_low, near_high = attend(core, near_q, kv, far, *outs, [size] * 2)
    after_low, before_high = join(after_low, before_high, from_low, from_high)
    low_1, high_2 = send(after_low, second_axis(1)), send(before_high, second_axis(-1))
    starts = [send(state, from_first(*to)) for to in ((0, 1), (1, 0), (1, 1))]
    total, to_minus, to_plus, to_opposite = split(
        [near_low, near_high, low_1, low_2, high_1, high_2], starts
    )
    arrived = [
        send(value, first_axis(s)) for value, s in ((to_plus, 1), (to_minus, -1), (to_opposite, 2))
    ]
    drift, term = drifts(index, step_sizes, total, arrived, gates)
    beside = send(term, to_other_core)
    earlier = send(both_cores(drift, beside), to_later_half)
    return finish(place, state, *starts, drift, beside, earlier)[None]


def solution(mesh):
    in_specs = (P("tm", "seq", None), P(None, None, "seq"), P("seq", None), P(), P(), P(), P(), P())
    out_specs = P("tm", "seq", None)
    return jax.shard_map(
        on_device, mesh=mesh, in_specs=in_specs, out_specs=out_specs, check_vma=False
    )
```

```python
import functools
import math

import jax
import jax.numpy as jnp
from jax import lax
from jax.experimental import pallas as pl
from jax.experimental.pallas import tpu as pltpu
from jax.sharding import PartitionSpec as P

HDIM = 128
XS, YLS, ZS = 4, 2, 4
BF16, F32 = jnp.bfloat16, jnp.float32
VMEM = pl.BlockSpec(memory_space=pltpu.VMEM)
SMEM = pl.BlockSpec(memory_space=pltpu.SMEM)
ANY = pl.BlockSpec(memory_space=pl.ANY)
PARAMS = pltpu.CompilerParams(vmem_limit_bytes=20 * 1024 * 1024)
WIDE = pltpu.CompilerParams(vmem_limit_bytes=60 * 1024 * 1024)


def moves(rule):
    pairs = []
    for yh in range(2):
        for core in range(2):
            for x in range(XS):
                for yl in range(YLS):
                    for z in range(ZS):
                        to = rule(yh, core, x, yl, z)
                        if to is not None:
                            pairs.append((flat(yh, core, x, yl, z), flat(*to)))
    return pairs


def flat(yh, core, x, yl, z):
    return (((yh * 2 + core) * XS + x) * YLS + yl) * ZS + z


def send(value, rule):
    return lax.ppermute(value, ("tm", "seq"), moves(rule))


def first_axis(step):
    return lambda yh, core, x, yl, z: (
        (yh, core, (x + step) % XS, yl, z) if core == 0 else (yh, core, x, yl, (z + step) % ZS)
    )


def second_axis(step):
    return lambda yh, core, x, yl, z: (
        (yh, core, x, yl, (z + step) % ZS) if core == 0 else (yh, core, (x + step) % XS, yl, z)
    )


def to_other_core(yh, core, x, yl, z):
    return (yh, 1 - core, x, yl, z)


def to_partner(yh, core, x, yl, z):
    return (yh, core, x, 1 - yl, z)


def to_both_sides(yh, core, x, yl, z):
    return (yh if core == 0 else 1 - yh, core, x, 1 - yl, z)


def to_later_half(yh, core, x, yl, z):
    return (1, core, x, yl, z) if yh == 0 else None


def to_later_core(yh, core, x, yl, z):
    return (0, 1, x, yl, z) if yh == 0 and core == 0 else None


def modulate_kernel(index, state, scale, shift, gate, out, gates):
    row = pl.ds(lax.rem(index[0], 8), 1)
    value = state[...]
    mean = jnp.mean(value * value, axis=-1, keepdims=True)
    normed = value * lax.rsqrt(mean + 1e-06)
    out[...] = (normed * (1.0 + scale[row, :]) + shift[row, :]).astype(BF16)
    gates[...] = gate[row, :]


def modulate(index, state, scale, shift, gate):
    rows, width = state.shape
    table = pl.BlockSpec((8, width), lambda i, index: (lax.div(index[0], 8), 0))
    whole = pl.BlockSpec((rows, width), lambda i, index: (0, 0))
    return pl.pallas_call(
        modulate_kernel,
        grid_spec=pltpu.PrefetchScalarGridSpec(
            num_scalar_prefetch=1,
            grid=(1,),
            in_specs=[whole, table, table, table],
            out_specs=[whole, pl.BlockSpec((1, width), lambda i, index: (0, 0))],
        ),
        out_shape=[
            jax.ShapeDtypeStruct(state.shape, BF16),
            jax.ShapeDtypeStruct((1, width), F32),
        ],
        compiler_params=WIDE,
        cost_estimate=pl.CostEstimate(flops=1000000, bytes_accessed=2000000, transcendentals=0),
    )(index, state, scale, shift, gate)


def pack_kernel(kinds, core, qkv, output, until, packed, sem):
    half = packed.shape[1]
    first = pl.multiple_of(core[0] * half, half)
    copies = []
    for place, kind in enumerate(kinds):
        if kind < 3:
            rows = qkv.at[kind, pl.ds(first, half), :]
            copies.append(pltpu.make_async_copy(rows, packed.at[place], sem))
        else:
            for at in range(0, half, HDIM):
                block = output.at[:, pl.ds(pl.multiple_of(first + at, HDIM), HDIM)]
                copies.append(
                    pltpu.make_async_copy(block, packed.at[place, pl.ds(at, HDIM), :], sem)
                )
    for copy in copies:
        copy.start()
    for copy in copies:
        copy.wait()


def pack(kinds, core, qkv_weight, out_weight, until):
    half = qkv_weight.shape[1] // 2
    return pl.pallas_call(
        functools.partial(pack_kernel, kinds),
        grid_spec=pltpu.PrefetchScalarGridSpec(
            num_scalar_prefetch=1,
            grid=(1,),
            in_specs=[ANY] * 3,
            out_specs=pl.BlockSpec((len(kinds), half, HDIM), lambda i, core: (0, 0, 0)),
            scratch_shapes=[pltpu.SemaphoreType.DMA],
        ),
        out_shape=jax.ShapeDtypeStruct((len(kinds), half, HDIM), BF16),
        compiler_params=PARAMS,
        cost_estimate=pl.CostEstimate(flops=0, bytes_accessed=4000000, transcendentals=0),
    )(core, qkv_weight, out_weight, until)


def stack_kernel(one, two, out):
    size = one.shape[0]
    out[:size] = one[...]
    out[size:] = two[...]


def stack(one, two):
    return pl.pallas_call(
        stack_kernel,
        out_shape=jax.ShapeDtypeStruct((2 * one.shape[0], one.shape[1]), one.dtype),
        in_specs=[VMEM] * 2,
        out_specs=VMEM,
        compiler_params=PARAMS,
    )(one, two)


def sides(core, mine, theirs, width, step, one):
    half = width // 2
    first = core[0] * half

    def side(weight, start):
        def body(block, carry):
            at = pl.multiple_of(block * step, step)
            one(weight, at, pl.multiple_of(start + at, 128))
            return carry

        lax.fori_loop(0, half // step, body, 0, unroll=True)

    side(mine, first)
    side(theirs, half - first)


def project_kernel(count, kinds, rows, core, *refs):
    pieces, (own, mine, theirs) = refs[:count], refs[count : count + 3]
    outs, total = refs[count + 3 : -1], refs[-1]
    step, wide = 512, 2 * HDIM
    total[...] = jnp.zeros_like(total)

    def one(weight, at, column):
        left = jnp.concatenate([piece[:, pl.ds(column, step)] for piece in pieces], axis=0)
        for place, kind in enumerate(kinds):
            both = jnp.concatenate(
                [own[kind, pl.ds(column, step), :], weight[place, pl.ds(at, step), :]], axis=-1
            )
            total[place] += jnp.dot(left, both, preferred_element_type=F32)

    sides(core, mine, theirs, own.shape[1], step, one)
    at = 0
    for out, size in zip(outs, rows):
        for place in range(len(kinds)):
            out[:, place * wide : (place + 1) * wide] = total[place, at : at + size].astype(BF16)
        at += size


def project(core, kinds, pieces, weight, mine, theirs, rows):
    wide = 2 * HDIM
    tokens, depth = sum(rows), weight.shape[1]
    return pl.pallas_call(
        functools.partial(project_kernel, len(pieces), kinds, rows),
        out_shape=[jax.ShapeDtypeStruct((size, len(kinds) * wide), BF16) for size in rows],
        in_specs=[SMEM] + [VMEM] * (len(pieces) + 3),
        out_specs=[VMEM] * len(rows),
        scratch_shapes=[pltpu.VMEM((len(kinds), tokens, wide), F32)],
        compiler_params=PARAMS,
        cost_estimate=pl.CostEstimate(
            flops=2 * len(kinds) * tokens * depth * wide, bytes_accessed=1000000, transcendentals=0
        ),
    )(core, *pieces, weight, mine, theirs)


def attend_kernel(count, cuts, core, queries, own, mine, theirs, *refs):
    near, far = refs[:count], refs[count : 2 * count]
    outs, attended = refs[2 * count : -1], refs[-1]
    scale = 1.0 / math.sqrt(HDIM)
    contract = (((1,), (1,)), ((), ()))
    for head in range(2):
        here = slice(head * HDIM, (head + 1) * HDIM)
        there = slice((1 - head) * HDIM, (2 - head) * HDIM)
        here_v = slice((2 + head) * HDIM, (3 + head) * HDIM)
        there_v = slice((3 - head) * HDIM, (4 - head) * HDIM)
        all_keys = jnp.concatenate([r[:, here] for r in near] + [r[:, there] for r in far], axis=0)
        all_values = jnp.concatenate(
            [r[:, here_v] for r in near] + [r[:, there_v] for r in far], axis=0
        )
        scores = lax.dot_general(queries[:, here], all_keys, contract, preferred_element_type=F32)
        top = jnp.max(scores, axis=-1, keepdims=True)
        weights = jnp.exp((scores - top) * scale)
        total = jnp.sum(weights, axis=-1, keepdims=True)
        mixed = jnp.dot(weights.astype(BF16), all_values, preferred_element_type=F32)
        attended[:, here] = (mixed / total).astype(BF16)
    step = 512

    def one(weight, at, column):
        blocks = [
            weight[1, pl.ds(pl.multiple_of(at + i, HDIM), HDIM), :] for i in range(0, step, HDIM)
        ]
        both = jnp.concatenate(
            [own[:, pl.ds(column, step)], jnp.concatenate(blocks, axis=1)], axis=0
        )
        result = jnp.dot(attended[...], both, preferred_element_type=F32).astype(BF16)
        row = 0
        for out, size in zip(outs, cuts):
            out[:, pl.ds(column, step)] = result[row : row + size]
            row += size

    sides(core, mine, theirs, own.shape[1], step, one)


def attend(core, queries, near, far, own, mine, theirs, cuts):
    width = own.shape[1]
    tokens = queries.shape[0]
    return pl.pallas_call(
        functools.partial(attend_kernel, len(near), cuts),
        out_shape=[jax.ShapeDtypeStruct((size, width), BF16) for size in cuts],
        in_specs=[SMEM] + [VMEM] * (4 + 2 * len(near)),
        out_specs=[VMEM] * len(cuts),
        scratch_shapes=[pltpu.VMEM((tokens, 2 * HDIM), BF16)],
        compiler_params=PARAMS,
        cost_estimate=pl.CostEstimate(
            flops=4 * tokens * HDIM * (width + 2048), bytes_accessed=1000000, transcendentals=0
        ),
    )(core, queries, own, mine, theirs, *near, *far)


def join_kernel(after, before, low, high, to_after, to_before):
    to_after[...] = (after[...].astype(F32) + low[...].astype(F32)).astype(BF16)
    to_before[...] = (before[...].astype(F32) + high[...].astype(F32)).astype(BF16)


def join(after, before, low, high):
    return pl.pallas_call(
        join_kernel,
        out_shape=[jax.ShapeDtypeStruct(before.shape, BF16)] * 2,
        in_specs=[VMEM] * 4,
        out_specs=[VMEM] * 2,
        compiler_params=PARAMS,
    )(after, before, low, high)


def split_kernel(*refs):
    near_low, near_high, low_1, low_2, high_1, high_2 = refs[:6]
    kept, to_minus, to_plus, to_opposite = refs[-4:]
    size = kept.shape[0]

    def total(near, one, two, rows):
        return near[rows].astype(F32) + one[rows].astype(F32) + two[rows].astype(F32)

    kept[...] = total(near_low, low_1, low_2, slice(0, size))
    to_minus[...] = total(near_low, low_1, low_2, slice(size, 2 * size)).astype(BF16)
    to_plus[...] = total(near_high, high_1, high_2, slice(0, size)).astype(BF16)
    to_opposite[...] = total(near_high, high_1, high_2, slice(size, 2 * size)).astype(BF16)


def split(*parts):
    size, width = parts[0].shape[0] // 2, parts[0].shape[1]
    return pl.pallas_call(
        split_kernel,
        out_shape=[jax.ShapeDtypeStruct((size, width), F32)]
        + [jax.ShapeDtypeStruct((size, width), BF16)] * 3,
        in_specs=[VMEM] * 6,
        out_specs=[VMEM] * 4,
        compiler_params=PARAMS,
    )(*parts)


def drift_kernel(index, steps, total, one, two, three, gates, *refs):
    drift, term = refs[-2:]
    moved = total[...] + one[...].astype(F32) + two[...].astype(F32) + three[...].astype(F32)
    result = steps[index[0]] * (gates[...] * moved)
    drift[...] = result
    term[...] = result.astype(BF16)


def drifts(index, steps, total, arrived, gates, *until):
    return pl.pallas_call(
        drift_kernel,
        out_shape=[
            jax.ShapeDtypeStruct(total.shape, F32),
            jax.ShapeDtypeStruct(total.shape, BF16),
        ],
        in_specs=[SMEM] * 2 + [VMEM] * 5 + [ANY] * len(until),
        out_specs=[VMEM] * 2,
        compiler_params=PARAMS,
    )(index, steps, total, *arrived, gates, *until)


def own_rows(place, half):
    return pl.ds(pl.multiple_of(lax.rem(place[0], 2) * half, half), half)


def start_kernel(place, state, received, until, out):
    rows = own_rows(place, out.shape[0])
    out[...] = jnp.where(place[0] == 0, state[rows, :], received[rows, :])


def start_half(place, state, received, until):
    return pl.pallas_call(
        start_kernel,
        out_shape=jax.ShapeDtypeStruct((state.shape[0] // 2, state.shape[1]), F32),
        in_specs=[SMEM] + [VMEM] * 2 + [ANY],
        out_specs=VMEM,
        compiler_params=PARAMS,
    )(place, state, received, until)


def both_kernel(place, drift, beside, out):
    rows = own_rows(place, out.shape[0])
    out[...] = (drift[rows, :] + beside[rows, :].astype(F32)).astype(BF16)


def both_half(place, drift, beside):
    return pl.pallas_call(
        both_kernel,
        out_shape=jax.ShapeDtypeStruct((drift.shape[0] // 2, drift.shape[1]), BF16),
        in_specs=[SMEM] + [VMEM] * 2,
        out_specs=VMEM,
        compiler_params=PARAMS,
    )(place, drift, beside)


def finish_kernel(place, state, near_start, own_start, far_start, drift, beside, own_sum, far_sum, out):
    half = own_sum.shape[0]
    second = lax.rem(place[0], 2)
    summed = drift[...] + jnp.where(second == 1, beside[...].astype(F32), 0.0)

    @pl.when(place[0] < 2)
    def _():
        out[...] = jnp.where(place[0] == 0, state[...], near_start[...]) + summed

    @pl.when(place[0] >= 2)
    def _():
        for which, start, earlier in ((0, own_start, own_sum), (1, far_start, far_sum)):
            rows = pl.ds(pl.multiple_of(lax.rem(second + which, 2) * half, half), half)
            out[rows, :] = start[...] + earlier[...].astype(F32)
        out[...] += summed


def finish(place, *parts):
    return pl.pallas_call(
        finish_kernel,
        out_shape=jax.ShapeDtypeStruct(parts[0].shape, F32),
        in_specs=[SMEM] + [VMEM] * 8,
        out_specs=VMEM,
        compiler_params=PARAMS,
    )(place, *parts)


def hold_kernel(value, *refs):
    del value, refs


def hold(value, *until):
    return pl.pallas_call(
        hold_kernel,
        out_shape=jax.ShapeDtypeStruct(value.shape, value.dtype),
        in_specs=[ANY] * (1 + len(until)),
        out_specs=ANY,
        input_output_aliases={0: 0},
        compiler_params=PARAMS,
    )(value, *until)


def on_device(
    trajectory, qkv_weight, out_weight, shift_table, scale_table, gate_table, step_sizes, window_start
):
    group = lax.axis_index("tm")
    core = group & 1
    place, core, index = group[None], core[None], window_start + group
    state = trajectory[0]
    modulated, gates = modulate(index, state, scale_table, shift_table, gate_table)
    near_start = send(state, to_later_core)
    minus, plus, opposite = [send(modulated, first_axis(s)) for s in (1, -1, 2)]
    near_low = stack(modulated, minus)
    before_low, after_low = send(near_low, second_axis(1)), send(near_low, second_axis(-1))
    near_high = stack(plus, opposite)
    after_high, before_high = send(near_high, second_axis(-1)), send(near_high, second_axis(1))
    kv_mine = send(pack((1, 2), core, qkv_weight, out_weight, modulated), to_both_sides)
    qo_mine = send(pack((0, 3), core, qkv_weight, out_weight, modulated), to_both_sides)
    last_low = send(hold(before_low, before_high, after_low), second_axis(1))
    last_high = send(hold(after_high, before_high, after_low), second_axis(-1))

    size = near_low.shape[0]
    near = [near_low, near_high]
    side = [before_low, before_high, after_low, after_high]
    last = [last_low, last_high]
    kv_mine = hold(kv_mine, near_low, near_high)
    kv_weights = (qkv_weight, kv_mine, send(kv_mine, to_other_core))
    qo_theirs = send(qo_mine, to_other_core)
    (first_kv,) = project(core, (1, 2), near + side, *kv_weights, [6 * size])
    (last_kv,) = project(core, (1, 2), last, *kv_weights, [2 * size])
    kv = [first_kv, last_kv]
    far = [send(value, to_partner) for value in kv]
    near_q, side_q, last_q = project(
        core,
        (0,),
        near + side + last,
        qkv_weight,
        qo_mine,
        qo_theirs,
        [2 * size, 4 * size, 2 * size],
    )

    outs = (out_weight, qo_mine, qo_theirs)
    last_low, last_high = attend(core, last_q, kv, far, *outs, [size] * 2)
    own_start = send(start_half(place, state, near_start, last_low), to_later_half)
    from_low, from_high = send(last_low, second_axis(1)), send(last_high, second_axis(-1))
    before_low, before_high, after_low, after_high = attend(
        core, side_q, kv, far, *outs, [size] * 4
    )
    high_1, low_2 = send(after_high, second_axis(1)), send(before_low, second_axis(-1))
    near_low, near_high = attend(core, near_q, kv, far, *outs, [size] * 2)
    after_low, before_high = join(after_low, before_high, from_low, from_high)
    low_1, high_2 = send(after_low, second_axis(1)), send(before_high, second_axis(-1))
    total, to_minus, to_plus, to_opposite = split(
        near_low, near_high, low_1, low_2, high_1, high_2
    )
    arrived = [
        send(value, first_axis(s)) for value, s in ((to_plus, 1), (to_minus, -1), (to_opposite, 2))
    ]
    far_start = send(own_start, to_other_core)
    drift, term = drifts(index, step_sizes, total, arrived, gates, far_start)
    beside = send(term, to_other_core)
    own_sum = send(both_half(place, drift, beside), to_later_half)
    far_sum = send(own_sum, to_other_core)
    return finish(
        place, state, near_start, own_start, far_start, drift, beside, own_sum, far_sum
    )[None]


def solution(mesh):
    in_specs = (P("tm", "seq", None), P(None, None, "seq"), P("seq", None), P(), P(), P(), P(), P())
    out_specs = P("tm", "seq", None)
    return jax.shard_map(
        on_device, mesh=mesh, in_specs=in_specs, out_specs=out_specs, check_vma=False
    )
```

```python
import functools
import math

import jax
import jax.numpy as jnp
from jax import lax
from jax.experimental import pallas as pl
from jax.experimental.pallas import tpu as pltpu
from jax.sharding import PartitionSpec as P

HDIM = 128
XS, YLS, ZS = 4, 2, 4
BF16, F32 = jnp.bfloat16, jnp.float32
VMEM = pl.BlockSpec(memory_space=pltpu.VMEM)
SMEM = pl.BlockSpec(memory_space=pltpu.SMEM)
ANY = pl.BlockSpec(memory_space=pl.ANY)
PARAMS = pltpu.CompilerParams(vmem_limit_bytes=20 * 1024 * 1024)
WIDE = pltpu.CompilerParams(vmem_limit_bytes=60 * 1024 * 1024)


def moves(rule):
    pairs = []
    for yh in range(2):
        for core in range(2):
            for x in range(XS):
                for yl in range(YLS):
                    for z in range(ZS):
                        to = rule(yh, core, x, yl, z)
                        if to is not None:
                            pairs.append((flat(yh, core, x, yl, z), flat(*to)))
    return pairs


def flat(yh, core, x, yl, z):
    return (((yh * 2 + core) * XS + x) * YLS + yl) * ZS + z


def send(value, rule):
    return lax.ppermute(value, ("tm", "seq"), moves(rule))


def first_axis(step):
    return lambda yh, core, x, yl, z: (
        (yh, core, (x + step) % XS, yl, z) if core == 0 else (yh, core, x, yl, (z + step) % ZS)
    )


def second_axis(step):
    return lambda yh, core, x, yl, z: (
        (yh, core, x, yl, (z + step) % ZS) if core == 0 else (yh, core, (x + step) % XS, yl, z)
    )


def to_other_core(yh, core, x, yl, z):
    return (yh, 1 - core, x, yl, z)


def to_partner(yh, core, x, yl, z):
    return (yh, core, x, 1 - yl, z)


def to_both_sides(yh, core, x, yl, z):
    return (yh if core == 0 else 1 - yh, core, x, 1 - yl, z)


def to_later_half(yh, core, x, yl, z):
    return (1, core, x, yl, z) if yh == 0 else None


def to_later_core(yh, core, x, yl, z):
    return (0, 1, x, yl, z) if yh == 0 and core == 0 else None


def modulate_kernel(index, state, scale, shift, gate, out, gates):
    row = pl.ds(lax.rem(index[0], 8), 1)
    value = state[...]
    mean = jnp.mean(value * value, axis=-1, keepdims=True)
    normed = value * lax.rsqrt(mean + 1e-06)
    out[...] = (normed * (1.0 + scale[row, :]) + shift[row, :]).astype(BF16)
    gates[...] = gate[row, :]


def modulate(index, state, scale, shift, gate):
    rows, width = state.shape
    table = pl.BlockSpec((8, width), lambda i, index: (lax.div(index[0], 8), 0))
    whole = pl.BlockSpec((rows, width), lambda i, index: (0, 0))
    return pl.pallas_call(
        modulate_kernel,
        grid_spec=pltpu.PrefetchScalarGridSpec(
            num_scalar_prefetch=1,
            grid=(1,),
            in_specs=[whole, table, table, table],
            out_specs=[whole, pl.BlockSpec((1, width), lambda i, index: (0, 0))],
        ),
        out_shape=[
            jax.ShapeDtypeStruct(state.shape, BF16),
            jax.ShapeDtypeStruct((1, width), F32),
        ],
        compiler_params=WIDE,
        cost_estimate=pl.CostEstimate(flops=1000000, bytes_accessed=2000000, transcendentals=0),
    )(index, state, scale, shift, gate)


def pack_kernel(kinds, core, qkv, *refs):
    packed, sem = refs[-2:]
    half = packed.shape[1]
    first = pl.multiple_of(core[0] * half, half)
    copies = []
    for place, kind in enumerate(kinds):
        if kind < 3:
            rows = qkv.at[kind, pl.ds(first, half), :]
            copies.append(pltpu.make_async_copy(rows, packed.at[place], sem))
        else:
            for at in range(0, half, HDIM):
                block = refs[0].at[:, pl.ds(pl.multiple_of(first + at, HDIM), HDIM)]
                copies.append(
                    pltpu.make_async_copy(block, packed.at[place, pl.ds(at, HDIM), :], sem)
                )
    for copy in copies:
        copy.start()
    for copy in copies:
        copy.wait()


def pack(kinds, core, qkv_weight, *more):
    half = qkv_weight.shape[1] // 2
    return pl.pallas_call(
        functools.partial(pack_kernel, kinds),
        grid_spec=pltpu.PrefetchScalarGridSpec(
            num_scalar_prefetch=1,
            grid=(1,),
            in_specs=[ANY] * (1 + len(more)),
            out_specs=pl.BlockSpec((len(kinds), half, HDIM), lambda i, core: (0, 0, 0)),
            scratch_shapes=[pltpu.SemaphoreType.DMA],
        ),
        out_shape=jax.ShapeDtypeStruct((len(kinds), half, HDIM), BF16),
        compiler_params=PARAMS,
        cost_estimate=pl.CostEstimate(flops=0, bytes_accessed=4000000, transcendentals=0),
    )(core, qkv_weight, *more)


def stack_kernel(*refs):
    out, at = refs[-1], 0
    for piece in refs[:-1]:
        out[at : at + piece.shape[0]] = piece[...]
        at += piece.shape[0]


def stack(*pieces):
    return pl.pallas_call(
        stack_kernel,
        out_shape=jax.ShapeDtypeStruct(
            (sum(piece.shape[0] for piece in pieces), pieces[0].shape[1]), BF16
        ),
        in_specs=[VMEM] * len(pieces),
        out_specs=VMEM,
        compiler_params=PARAMS,
    )(*pieces)


def halves_kernel(one, two, *refs):
    low, high = refs[-2:]
    half = low.shape[0]
    low[...] = one[:half]
    high[...] = two[half:]


def first_and_second_half(one, two, *until):
    return pl.pallas_call(
        halves_kernel,
        out_shape=[jax.ShapeDtypeStruct((one.shape[0] // 2, one.shape[1]), BF16)] * 2,
        in_specs=[VMEM] * 2 + [ANY] * len(until),
        out_specs=[VMEM] * 2,
        compiler_params=PARAMS,
    )(one, two, *until)


def sides(core, mine, theirs, width, step, one):
    half = width // 2
    first = core[0] * half

    def side(weight, start):
        def body(block, carry):
            at = pl.multiple_of(block * step, step)
            one(weight, at, pl.multiple_of(start + at, 128))
            return carry

        lax.fori_loop(0, half // step, body, 0, unroll=True)

    side(mine, first)
    side(theirs, half - first)


def project_kernel(count, kinds, rows, core, *refs):
    pieces, (own, mine, theirs) = refs[:count], refs[count : count + 3]
    outs, total = refs[count + 3 : -1], refs[-1]
    step, wide = 512, 2 * HDIM
    total[...] = jnp.zeros_like(total)

    def one(weight, at, column):
        left = jnp.concatenate([piece[:, pl.ds(column, step)] for piece in pieces], axis=0)
        for place, kind in enumerate(kinds):
            both = jnp.concatenate(
                [own[kind, pl.ds(column, step), :], weight[place, pl.ds(at, step), :]], axis=-1
            )
            total[place] += jnp.dot(left, both, preferred_element_type=F32)

    sides(core, mine, theirs, own.shape[1], step, one)
    at = 0
    for out, size in zip(outs, rows):
        for place in range(len(kinds)):
            out[:, place * wide : (place + 1) * wide] = total[place, at : at + size].astype(BF16)
        at += size


def project(core, kinds, pieces, weight, mine, theirs, rows):
    wide = 2 * HDIM
    tokens, depth = sum(rows), weight.shape[1]
    return pl.pallas_call(
        functools.partial(project_kernel, len(pieces), kinds, rows),
        out_shape=[jax.ShapeDtypeStruct((size, len(kinds) * wide), BF16) for size in rows],
        in_specs=[SMEM] + [VMEM] * (len(pieces) + 3),
        out_specs=[VMEM] * len(rows),
        scratch_shapes=[pltpu.VMEM((len(kinds), tokens, wide), F32)],
        compiler_params=PARAMS,
        cost_estimate=pl.CostEstimate(
            flops=2 * len(kinds) * tokens * depth * wide, bytes_accessed=1000000, transcendentals=0
        ),
    )(core, *pieces, weight, mine, theirs)


def attend_kernel(count, cuts, core, queries, own, mine, theirs, *refs):
    near, far = refs[:count], refs[count : 2 * count]
    outs, attended = refs[2 * count : -1], refs[-1]
    scale = 1.0 / math.sqrt(HDIM)
    contract = (((1,), (1,)), ((), ()))
    for head in range(2):
        here = slice(head * HDIM, (head + 1) * HDIM)
        there = slice((1 - head) * HDIM, (2 - head) * HDIM)
        here_v = slice((2 + head) * HDIM, (3 + head) * HDIM)
        there_v = slice((3 - head) * HDIM, (4 - head) * HDIM)
        all_keys = jnp.concatenate([r[:, here] for r in near] + [r[:, there] for r in far], axis=0)
        all_values = jnp.concatenate(
            [r[:, here_v] for r in near] + [r[:, there_v] for r in far], axis=0
        )
        scores = lax.dot_general(queries[:, here], all_keys, contract, preferred_element_type=F32)
        top = jnp.max(scores, axis=-1, keepdims=True)
        weights = jnp.exp((scores - top) * scale)
        total = jnp.sum(weights, axis=-1, keepdims=True)
        mixed = jnp.dot(weights.astype(BF16), all_values, preferred_element_type=F32)
        attended[:, here] = (mixed / total).astype(BF16)
    step = 512

    def one(weight, at, column):
        blocks = [
            weight[1, pl.ds(pl.multiple_of(at + i, HDIM), HDIM), :] for i in range(0, step, HDIM)
        ]
        both = jnp.concatenate(
            [own[:, pl.ds(column, step)], jnp.concatenate(blocks, axis=1)], axis=0
        )
        result = jnp.dot(attended[...], both, preferred_element_type=F32).astype(BF16)
        row = 0
        for out, size in zip(outs, cuts):
            out[:, pl.ds(column, step)] = result[row : row + size]
            row += size

    sides(core, mine, theirs, own.shape[1], step, one)


def attend(core, queries, near, far, own, mine, theirs, cuts):
    width = own.shape[1]
    tokens = queries.shape[0]
    return pl.pallas_call(
        functools.partial(attend_kernel, len(near), cuts),
        out_shape=[jax.ShapeDtypeStruct((size, width), BF16) for size in cuts],
        in_specs=[SMEM] + [VMEM] * (4 + 2 * len(near)),
        out_specs=[VMEM] * len(cuts),
        scratch_shapes=[pltpu.VMEM((tokens, 2 * HDIM), BF16)],
        compiler_params=PARAMS,
        cost_estimate=pl.CostEstimate(
            flops=4 * tokens * HDIM * (width + 2048), bytes_accessed=1000000, transcendentals=0
        ),
    )(core, queries, own, mine, theirs, *near, *far)


def join_kernel(after, before, low, high, to_after, to_before):
    to_after[...] = (after[...].astype(F32) + low[...].astype(F32)).astype(BF16)
    to_before[...] = (before[...].astype(F32) + high[...].astype(F32)).astype(BF16)


def join(after, before, low, high):
    return pl.pallas_call(
        join_kernel,
        out_shape=[jax.ShapeDtypeStruct(before.shape, BF16)] * 2,
        in_specs=[VMEM] * 4,
        out_specs=[VMEM] * 2,
        compiler_params=PARAMS,
    )(after, before, low, high)


def split_kernel(*refs):
    near_low, near_high, low_1, low_2, high_1, high_2 = refs[:6]
    kept, to_minus, to_plus, to_opposite = refs[-4:]
    size = kept.shape[0]

    def total(near, one, two, rows):
        return near[rows].astype(F32) + one[rows].astype(F32) + two[rows].astype(F32)

    kept[...] = total(near_low, low_1, low_2, slice(0, size))
    to_minus[...] = total(near_low, low_1, low_2, slice(size, 2 * size)).astype(BF16)
    to_plus[...] = total(near_high, high_1, high_2, slice(0, size)).astype(BF16)
    to_opposite[...] = total(near_high, high_1, high_2, slice(size, 2 * size)).astype(BF16)


def split(*parts):
    size, width = parts[0].shape[0] // 2, parts[0].shape[1]
    return pl.pallas_call(
        split_kernel,
        out_shape=[jax.ShapeDtypeStruct((size, width), F32)]
        + [jax.ShapeDtypeStruct((size, width), BF16)] * 3,
        in_specs=[VMEM] * 6,
        out_specs=[VMEM] * 4,
        compiler_params=PARAMS,
    )(*parts)


def drift_kernel(index, steps, total, one, two, three, gates, *refs):
    drift, term = refs[-2:]
    moved = total[...] + one[...].astype(F32) + two[...].astype(F32) + three[...].astype(F32)
    result = steps[index[0]] * (gates[...] * moved)
    drift[...] = result
    term[...] = result.astype(BF16)


def drifts(index, steps, total, arrived, gates, *until):
    return pl.pallas_call(
        drift_kernel,
        out_shape=[
            jax.ShapeDtypeStruct(total.shape, F32),
            jax.ShapeDtypeStruct(total.shape, BF16),
        ],
        in_specs=[SMEM] * 2 + [VMEM] * 5 + [ANY] * len(until),
        out_specs=[VMEM] * 2,
        compiler_params=PARAMS,
    )(index, steps, total, *arrived, gates, *until)


def own_rows(place, half):
    return pl.ds(pl.multiple_of(lax.rem(place[0], 2) * half, half), half)


def start_kernel(place, state, received, until, out):
    rows = own_rows(place, out.shape[0])
    out[...] = jnp.where(place[0] == 0, state[rows, :], received[rows, :])


def start_half(place, state, received, until):
    return pl.pallas_call(
        start_kernel,
        out_shape=jax.ShapeDtypeStruct((state.shape[0] // 2, state.shape[1]), F32),
        in_specs=[SMEM] + [VMEM] * 2 + [ANY],
        out_specs=VMEM,
        compiler_params=PARAMS,
    )(place, state, received, until)


def both_kernel(place, drift, beside, out):
    rows = own_rows(place, out.shape[0])
    out[...] = (drift[rows, :] + beside[rows, :].astype(F32)).astype(BF16)


def both_half(place, drift, beside):
    return pl.pallas_call(
        both_kernel,
        out_shape=jax.ShapeDtypeStruct((drift.shape[0] // 2, drift.shape[1]), BF16),
        in_specs=[SMEM] + [VMEM] * 2,
        out_specs=VMEM,
        compiler_params=PARAMS,
    )(place, drift, beside)


def finish_kernel(place, state, near_start, own_start, far_start, drift, beside, own_sum, far_sum, out):
    half = own_sum.shape[0]
    second = lax.rem(place[0], 2)
    summed = drift[...] + jnp.where(second == 1, beside[...].astype(F32), 0.0)

    @pl.when(place[0] < 2)
    def _():
        out[...] = jnp.where(place[0] == 0, state[...], near_start[...]) + summed

    @pl.when(place[0] >= 2)
    def _():
        for which, start, earlier in ((0, own_start, own_sum), (1, far_start, far_sum)):
            rows = pl.ds(pl.multiple_of(lax.rem(second + which, 2) * half, half), half)
            out[rows, :] = start[...] + earlier[...].astype(F32)
        out[...] += summed


def finish(place, *parts):
    return pl.pallas_call(
        finish_kernel,
        out_shape=jax.ShapeDtypeStruct(parts[0].shape, F32),
        in_specs=[SMEM] + [VMEM] * 8,
        out_specs=VMEM,
        compiler_params=PARAMS,
    )(place, *parts)


def hold_kernel(value, *refs):
    del value, refs


def hold(value, *until):
    return pl.pallas_call(
        hold_kernel,
        out_shape=jax.ShapeDtypeStruct(value.shape, value.dtype),
        in_specs=[ANY] * (1 + len(until)),
        out_specs=ANY,
        input_output_aliases={0: 0},
        compiler_params=PARAMS,
    )(value, *until)


def on_device(
    trajectory, qkv_weight, out_weight, shift_table, scale_table, gate_table, step_sizes, window_start
):
    group = lax.axis_index("tm")
    core = group & 1
    place, core, index = group[None], core[None], window_start + group
    state = trajectory[0]
    modulated, gates = modulate(index, state, scale_table, shift_table, gate_table)
    near_start = send(state, to_later_core)
    minus, plus, opposite = [send(modulated, first_axis(s)) for s in (1, -1, 2)]
    near = stack(modulated, minus, plus, opposite)
    before, after = send(near, second_axis(1)), send(near, second_axis(-1))
    kv_mine = send(pack((1, 2), core, qkv_weight, modulated), to_both_sides)
    qo_mine = send(pack((0, 3), core, qkv_weight, out_weight, minus, plus, opposite), to_both_sides)
    before_half, after_half = first_and_second_half(before, after, near_start)
    last = [send(before_half, second_axis(1)), send(after_half, second_axis(-1))]

    size = before_half.shape[0]
    kv_mine = hold(kv_mine, near)
    kv_weights = (qkv_weight, kv_mine, send(kv_mine, to_other_core))
    qo_theirs = send(qo_mine, to_other_core)
    (first_kv,) = project(core, (1, 2), [near, before, after], *kv_weights, [6 * size])
    (last_kv,) = project(core, (1, 2), last, *kv_weights, [2 * size])
    kv = [first_kv, last_kv]
    far = [send(value, to_partner) for value in kv]
    near_q, side_q, last_q = project(
        core,
        (0,),
        [near, before, after, *last],
        qkv_weight,
        qo_mine,
        qo_theirs,
        [2 * size, 4 * size, 2 * size],
    )

    outs = (out_weight, qo_mine, qo_theirs)
    last_low, last_high = attend(core, last_q, kv, far, *outs, [size] * 2)
    own_start = send(start_half(place, state, near_start, last_low), to_later_half)
    from_low, from_high = send(last_low, second_axis(1)), send(last_high, second_axis(-1))
    before_low, before_high, after_low, after_high = attend(
        core, side_q, kv, far, *outs, [size] * 4
    )
    high_1, low_2 = send(after_high, second_axis(1)), send(before_low, second_axis(-1))
    near_low, near_high = attend(core, near_q, kv, far, *outs, [size] * 2)
    after_low, before_high = join(after_low, before_high, from_low, from_high)
    low_1, high_2 = send(after_low, second_axis(1)), send(before_high, second_axis(-1))
    total, to_minus, to_plus, to_opposite = split(
        near_low, near_high, low_1, low_2, high_1, high_2
    )
    arrived = [
        send(value, first_axis(s)) for value, s in ((to_plus, 1), (to_minus, -1), (to_opposite, 2))
    ]
    far_start = send(own_start, to_other_core)
    drift, term = drifts(index, step_sizes, total, arrived, gates, far_start)
    beside = send(term, to_other_core)
    own_sum = send(both_half(place, drift, beside), to_later_half)
    far_sum = send(own_sum, to_other_core)
    return finish(
        place, state, near_start, own_start, far_start, drift, beside, own_sum, far_sum
    )[None]


def solution(mesh):
    in_specs = (P("tm", "seq", None), P(None, None, "seq"), P("seq", None), P(), P(), P(), P(), P())
    out_specs = P("tm", "seq", None)
    return jax.shard_map(
        on_device, mesh=mesh, in_specs=in_specs, out_specs=out_specs, check_vma=False
    )
```

```python
import functools
import math

import jax
import jax.numpy as jnp
from jax import lax
from jax.experimental import pallas as pl
from jax.experimental.pallas import tpu as pltpu
from jax.sharding import PartitionSpec as P

HDIM = 128
XS, YLS, ZS = 4, 2, 4
BF16, F32 = jnp.bfloat16, jnp.float32
VMEM = pl.BlockSpec(memory_space=pltpu.VMEM)
SMEM = pl.BlockSpec(memory_space=pltpu.SMEM)
ANY = pl.BlockSpec(memory_space=pl.ANY)
PARAMS = pltpu.CompilerParams(vmem_limit_bytes=20 * 1024 * 1024)
WIDE = pltpu.CompilerParams(vmem_limit_bytes=60 * 1024 * 1024)


def moves(rule):
    pairs = []
    for yh in range(2):
        for core in range(2):
            for x in range(XS):
                for yl in range(YLS):
                    for z in range(ZS):
                        to = rule(yh, core, x, yl, z)
                        if to is not None:
                            pairs.append((flat(yh, core, x, yl, z), flat(*to)))
    return pairs


def flat(yh, core, x, yl, z):
    return (((yh * 2 + core) * XS + x) * YLS + yl) * ZS + z


def send(value, rule):
    return lax.ppermute(value, ("tm", "seq"), moves(rule))


def first_axis(step):
    return lambda yh, core, x, yl, z: (
        (yh, core, (x + step) % XS, yl, z) if core == 0 else (yh, core, x, yl, (z + step) % ZS)
    )


def second_axis(step):
    return lambda yh, core, x, yl, z: (
        (yh, core, x, yl, (z + step) % ZS) if core == 0 else (yh, core, (x + step) % XS, yl, z)
    )


def to_other_core(yh, core, x, yl, z):
    return (yh, 1 - core, x, yl, z)


def to_partner(yh, core, x, yl, z):
    return (yh, core, x, 1 - yl, z)


def to_both_sides(yh, core, x, yl, z):
    return (yh if core == 0 else 1 - yh, core, x, 1 - yl, z)


def to_other_half(yh, core, x, yl, z):
    return (1 - yh, core, x, yl, z)


def modulate_kernel(index, state, scale, shift, gate, out, gates):
    row = pl.ds(lax.rem(index[0], 8), 1)
    value = state[...]
    mean = jnp.mean(value * value, axis=-1, keepdims=True)
    normed = value * lax.rsqrt(mean + 1e-06)
    out[...] = (normed * (1.0 + scale[row, :]) + shift[row, :]).astype(BF16)
    gates[...] = gate[row, :]


def modulate(index, state, scale, shift, gate):
    rows, width = state.shape
    table = pl.BlockSpec((8, width), lambda i, index: (lax.div(index[0], 8), 0))
    whole = pl.BlockSpec((rows, width), lambda i, index: (0, 0))
    return pl.pallas_call(
        modulate_kernel,
        grid_spec=pltpu.PrefetchScalarGridSpec(
            num_scalar_prefetch=1,
            grid=(1,),
            in_specs=[whole, table, table, table],
            out_specs=[whole, pl.BlockSpec((1, width), lambda i, index: (0, 0))],
        ),
        out_shape=[
            jax.ShapeDtypeStruct(state.shape, BF16),
            jax.ShapeDtypeStruct((1, width), F32),
        ],
        compiler_params=WIDE,
        cost_estimate=pl.CostEstimate(flops=1000000, bytes_accessed=2000000, transcendentals=0),
    )(index, state, scale, shift, gate)


def pack_kernel(kinds, core, qkv, *refs):
    packed, sem = refs[-2:]
    half = packed.shape[1]
    first = pl.multiple_of(core[0] * half, half)
    copies = []
    for place, kind in enumerate(kinds):
        if kind < 3:
            rows = qkv.at[kind, pl.ds(first, half), :]
            copies.append(pltpu.make_async_copy(rows, packed.at[place], sem))
        else:
            for at in range(0, half, HDIM):
                block = refs[0].at[:, pl.ds(pl.multiple_of(first + at, HDIM), HDIM)]
                copies.append(
                    pltpu.make_async_copy(block, packed.at[place, pl.ds(at, HDIM), :], sem)
                )
    for copy in copies:
        copy.start()
    for copy in copies:
        copy.wait()


def pack(kinds, core, qkv_weight, *more):
    half = qkv_weight.shape[1] // 2
    return pl.pallas_call(
        functools.partial(pack_kernel, kinds),
        grid_spec=pltpu.PrefetchScalarGridSpec(
            num_scalar_prefetch=1,
            grid=(1,),
            in_specs=[ANY] * (1 + len(more)),
            out_specs=pl.BlockSpec((len(kinds), half, HDIM), lambda i, core: (0, 0, 0)),
            scratch_shapes=[pltpu.SemaphoreType.DMA],
        ),
        out_shape=jax.ShapeDtypeStruct((len(kinds), half, HDIM), BF16),
        compiler_params=PARAMS,
        cost_estimate=pl.CostEstimate(flops=0, bytes_accessed=4000000, transcendentals=0),
    )(core, qkv_weight, *more)


def stack_kernel(*refs):
    out, at = refs[-1], 0
    for piece in refs[:-1]:
        out[at : at + piece.shape[0]] = piece[...]
        at += piece.shape[0]


def stack(*pieces):
    return pl.pallas_call(
        stack_kernel,
        out_shape=jax.ShapeDtypeStruct(
            (sum(piece.shape[0] for piece in pieces), pieces[0].shape[1]), BF16
        ),
        in_specs=[VMEM] * len(pieces),
        out_specs=VMEM,
        compiler_params=PARAMS,
    )(*pieces)


def halves_kernel(one, two, *refs):
    low, high = refs[-2:]
    half = low.shape[0]
    low[...] = one[:half]
    high[...] = two[half:]


def first_and_second_half(one, two, *until):
    return pl.pallas_call(
        halves_kernel,
        out_shape=[jax.ShapeDtypeStruct((one.shape[0] // 2, one.shape[1]), BF16)] * 2,
        in_specs=[VMEM] * 2 + [ANY] * len(until),
        out_specs=[VMEM] * 2,
        compiler_params=PARAMS,
    )(one, two, *until)


def sides(core, mine, theirs, width, step, one):
    half = width // 2
    first = core[0] * half

    def side(weight, start):
        def body(block, carry):
            at = pl.multiple_of(block * step, step)
            one(weight, at, pl.multiple_of(start + at, 128))
            return carry

        lax.fori_loop(0, half // step, body, 0, unroll=True)

    side(mine, first)
    side(theirs, half - first)


def project_kernel(count, kinds, rows, core, *refs):
    pieces, (own, mine, theirs) = refs[:count], refs[count : count + 3]
    outs, total = refs[count + 3 : -1], refs[-1]
    step, wide = 512, 2 * HDIM
    total[...] = jnp.zeros_like(total)

    def one(weight, at, column):
        left = jnp.concatenate([piece[:, pl.ds(column, step)] for piece in pieces], axis=0)
        for place, kind in enumerate(kinds):
            both = jnp.concatenate(
                [own[kind, pl.ds(column, step), :], weight[place, pl.ds(at, step), :]], axis=-1
            )
            total[place] += jnp.dot(left, both, preferred_element_type=F32)

    sides(core, mine, theirs, own.shape[1], step, one)
    at = 0
    for out, size in zip(outs, rows):
        for place in range(len(kinds)):
            out[:, place * wide : (place + 1) * wide] = total[place, at : at + size].astype(BF16)
        at += size


def project(core, kinds, pieces, weight, mine, theirs, rows):
    wide = 2 * HDIM
    tokens, depth = sum(rows), weight.shape[1]
    return pl.pallas_call(
        functools.partial(project_kernel, len(pieces), kinds, rows),
        out_shape=[jax.ShapeDtypeStruct((size, len(kinds) * wide), BF16) for size in rows],
        in_specs=[SMEM] + [VMEM] * (len(pieces) + 3),
        out_specs=[VMEM] * len(rows),
        scratch_shapes=[pltpu.VMEM((len(kinds), tokens, wide), F32)],
        compiler_params=PARAMS,
        cost_estimate=pl.CostEstimate(
            flops=2 * len(kinds) * tokens * depth * wide, bytes_accessed=1000000, transcendentals=0
        ),
    )(core, *pieces, weight, mine, theirs)


def attend_kernel(count, cuts, core, queries, own, mine, theirs, *refs):
    near, far = refs[:count], refs[count : 2 * count]
    outs, attended = refs[2 * count : -1], refs[-1]
    scale = 1.0 / math.sqrt(HDIM)
    contract = (((1,), (1,)), ((), ()))
    for head in range(2):
        here = slice(head * HDIM, (head + 1) * HDIM)
        there = slice((1 - head) * HDIM, (2 - head) * HDIM)
        here_v = slice((2 + head) * HDIM, (3 + head) * HDIM)
        there_v = slice((3 - head) * HDIM, (4 - head) * HDIM)
        all_keys = jnp.concatenate([r[:, here] for r in near] + [r[:, there] for r in far], axis=0)
        all_values = jnp.concatenate(
            [r[:, here_v] for r in near] + [r[:, there_v] for r in far], axis=0
        )
        scores = lax.dot_general(queries[:, here], all_keys, contract, preferred_element_type=F32)
        top = jnp.max(scores, axis=-1, keepdims=True)
        weights = jnp.exp((scores - top) * scale)
        total = jnp.sum(weights, axis=-1, keepdims=True)
        mixed = jnp.dot(weights.astype(BF16), all_values, preferred_element_type=F32)
        attended[:, here] = (mixed / total).astype(BF16)
    step = 512

    def one(weight, at, column):
        blocks = [
            weight[1, pl.ds(pl.multiple_of(at + i, HDIM), HDIM), :] for i in range(0, step, HDIM)
        ]
        both = jnp.concatenate(
            [own[:, pl.ds(column, step)], jnp.concatenate(blocks, axis=1)], axis=0
        )
        result = jnp.dot(attended[...], both, preferred_element_type=F32).astype(BF16)
        row = 0
        for out, size in zip(outs, cuts):
            out[:, pl.ds(column, step)] = result[row : row + size]
            row += size

    sides(core, mine, theirs, own.shape[1], step, one)


def attend(core, queries, near, far, own, mine, theirs, cuts):
    width = own.shape[1]
    tokens = queries.shape[0]
    return pl.pallas_call(
        functools.partial(attend_kernel, len(near), cuts),
        out_shape=[jax.ShapeDtypeStruct((size, width), BF16) for size in cuts],
        in_specs=[SMEM] + [VMEM] * (4 + 2 * len(near)),
        out_specs=[VMEM] * len(cuts),
        scratch_shapes=[pltpu.VMEM((tokens, 2 * HDIM), BF16)],
        compiler_params=PARAMS,
        cost_estimate=pl.CostEstimate(
            flops=4 * tokens * HDIM * (width + 2048), bytes_accessed=1000000, transcendentals=0
        ),
    )(core, queries, own, mine, theirs, *near, *far)


def join_kernel(after, before, low, high, to_after, to_before):
    to_after[...] = (after[...].astype(F32) + low[...].astype(F32)).astype(BF16)
    to_before[...] = (before[...].astype(F32) + high[...].astype(F32)).astype(BF16)


def join(after, before, low, high):
    return pl.pallas_call(
        join_kernel,
        out_shape=[jax.ShapeDtypeStruct(before.shape, BF16)] * 2,
        in_specs=[VMEM] * 4,
        out_specs=[VMEM] * 2,
        compiler_params=PARAMS,
    )(after, before, low, high)


def split_kernel(*refs):
    near_low, near_high, low_1, low_2, high_1, high_2 = refs[:6]
    kept, to_minus, to_plus, to_opposite = refs[-4:]
    size = kept.shape[0]

    def total(near, one, two, rows):
        return near[rows].astype(F32) + one[rows].astype(F32) + two[rows].astype(F32)

    kept[...] = total(near_low, low_1, low_2, slice(0, size))
    to_minus[...] = total(near_low, low_1, low_2, slice(size, 2 * size)).astype(BF16)
    to_plus[...] = total(near_high, high_1, high_2, slice(0, size)).astype(BF16)
    to_opposite[...] = total(near_high, high_1, high_2, slice(size, 2 * size)).astype(BF16)


def split(*parts):
    size, width = parts[0].shape[0] // 2, parts[0].shape[1]
    return pl.pallas_call(
        split_kernel,
        out_shape=[jax.ShapeDtypeStruct((size, width), F32)]
        + [jax.ShapeDtypeStruct((size, width), BF16)] * 3,
        in_specs=[VMEM] * 6,
        out_specs=[VMEM] * 4,
        compiler_params=PARAMS,
    )(*parts)


def drift_kernel(index, steps, total, one, two, three, gates, *refs):
    drift, term = refs[-2:]
    moved = total[...] + one[...].astype(F32) + two[...].astype(F32) + three[...].astype(F32)
    result = steps[index[0]] * (gates[...] * moved)
    drift[...] = result
    term[...] = result.astype(BF16)


def drifts(index, steps, total, arrived, gates, *until):
    return pl.pallas_call(
        drift_kernel,
        out_shape=[
            jax.ShapeDtypeStruct(total.shape, F32),
            jax.ShapeDtypeStruct(total.shape, BF16),
        ],
        in_specs=[SMEM] * 2 + [VMEM] * 5 + [ANY] * len(until),
        out_specs=[VMEM] * 2,
        compiler_params=PARAMS,
    )(index, steps, total, *arrived, gates, *until)


def own_rows(place, half):
    return pl.ds(pl.multiple_of(lax.rem(place[0], 2) * half, half), half)


def start_kernel(place, state, received, until, out):
    rows = own_rows(place, out.shape[0])
    out[...] = jnp.where(place[0] == 0, state[rows, :], received[rows, :])


def start_half(place, state, received, until):
    return pl.pallas_call(
        start_kernel,
        out_shape=jax.ShapeDtypeStruct((state.shape[0] // 2, state.shape[1]), F32),
        in_specs=[SMEM] + [VMEM] * 2 + [ANY],
        out_specs=VMEM,
        compiler_params=PARAMS,
    )(place, state, received, until)


def both_kernel(place, drift, beside, out):
    rows = own_rows(place, out.shape[0])
    out[...] = (drift[rows, :] + beside[rows, :].astype(F32)).astype(BF16)


def both_half(place, drift, beside):
    return pl.pallas_call(
        both_kernel,
        out_shape=jax.ShapeDtypeStruct((drift.shape[0] // 2, drift.shape[1]), BF16),
        in_specs=[SMEM] + [VMEM] * 2,
        out_specs=VMEM,
        compiler_params=PARAMS,
    )(place, drift, beside)


def finish_kernel(place, state, near_start, own_start, far_start, drift, beside, own_sum, far_sum, out):
    half = own_sum.shape[0]
    second = lax.rem(place[0], 2)
    summed = drift[...] + jnp.where(second == 1, beside[...].astype(F32), 0.0)

    @pl.when(place[0] < 2)
    def _():
        out[...] = jnp.where(place[0] == 0, state[...], near_start[...]) + summed

    @pl.when(place[0] >= 2)
    def _():
        for which, start, earlier in ((0, own_start, own_sum), (1, far_start, far_sum)):
            rows = pl.ds(pl.multiple_of(lax.rem(second + which, 2) * half, half), half)
            out[rows, :] = start[...] + earlier[...].astype(F32)
        out[...] += summed


def finish(place, *parts):
    return pl.pallas_call(
        finish_kernel,
        out_shape=jax.ShapeDtypeStruct(parts[0].shape, F32),
        in_specs=[SMEM] + [VMEM] * 8,
        out_specs=VMEM,
        compiler_params=PARAMS,
    )(place, *parts)


def hold_kernel(value, *refs):
    del value, refs


def hold(value, *until):
    return pl.pallas_call(
        hold_kernel,
        out_shape=jax.ShapeDtypeStruct(value.shape, value.dtype),
        in_specs=[ANY] * (1 + len(until)),
        out_specs=ANY,
        input_output_aliases={0: 0},
        compiler_params=PARAMS,
    )(value, *until)


def on_device(
    trajectory, qkv_weight, out_weight, shift_table, scale_table, gate_table, step_sizes, window_start
):
    group = lax.axis_index("tm")
    core = group & 1
    place, core, index = group[None], core[None], window_start + group
    state = trajectory[0]
    modulated, gates = modulate(index, state, scale_table, shift_table, gate_table)
    near_start = send(state, to_other_core)
    minus, plus, opposite = [send(modulated, first_axis(s)) for s in (1, -1, 2)]
    near = stack(modulated, minus, plus, opposite)
    before, after = send(near, second_axis(1)), send(near, second_axis(-1))
    kv_mine = send(pack((1, 2), core, qkv_weight, modulated), to_both_sides)
    qo_mine = send(pack((0, 3), core, qkv_weight, out_weight, minus, plus, opposite), to_both_sides)
    before_half, after_half = first_and_second_half(before, after, near_start)
    last = [send(before_half, second_axis(1)), send(after_half, second_axis(-1))]

    size = before_half.shape[0]
    kv_mine = hold(kv_mine, near)
    kv_weights = (qkv_weight, kv_mine, send(kv_mine, to_other_core))
    qo_theirs = send(qo_mine, to_other_core)
    (first_kv,) = project(core, (1, 2), [near, before, after], *kv_weights, [6 * size])
    (last_kv,) = project(core, (1, 2), last, *kv_weights, [2 * size])
    kv = [first_kv, last_kv]
    far = [send(value, to_partner) for value in kv]
    near_q, side_q, last_q = project(
        core,
        (0,),
        [near, before, after, *last],
        qkv_weight,
        qo_mine,
        qo_theirs,
        [2 * size, 4 * size, 2 * size],
    )

    outs = (out_weight, qo_mine, qo_theirs)
    last_low, last_high = attend(core, last_q, kv, far, *outs, [size] * 2)
    own_start = send(start_half(place, state, near_start, last_low), to_other_half)
    from_low, from_high = send(last_low, second_axis(1)), send(last_high, second_axis(-1))
    before_low, before_high, after_low, after_high = attend(
        core, side_q, kv, far, *outs, [size] * 4
    )
    high_1, low_2 = send(after_high, second_axis(1)), send(before_low, second_axis(-1))
    near_low, near_high = attend(core, near_q, kv, far, *outs, [size] * 2)
    after_low, before_high = join(after_low, before_high, from_low, from_high)
    low_1, high_2 = send(after_low, second_axis(1)), send(before_high, second_axis(-1))
    total, to_minus, to_plus, to_opposite = split(
        near_low, near_high, low_1, low_2, high_1, high_2
    )
    arrived = [
        send(value, first_axis(s)) for value, s in ((to_opposite, 2), (to_plus, 1), (to_minus, -1))
    ]
    far_start = send(own_start, to_other_core)
    drift, term = drifts(index, step_sizes, total, arrived, gates, far_start)
    beside = send(term, to_other_core)
    own_sum = send(both_half(place, drift, beside), to_other_half)
    far_sum = send(own_sum, to_other_core)
    return finish(
        place, state, near_start, own_start, far_start, drift, beside, own_sum, far_sum
    )[None]


def solution(mesh):
    in_specs = (P("tm", "seq", None), P(None, None, "seq"), P("seq", None), P(), P(), P(), P(), P())
    out_specs = P("tm", "seq", None)
    return jax.shard_map(
        on_device, mesh=mesh, in_specs=in_specs, out_specs=out_specs, check_vma=False
    )
```

```python
import functools
import math

import jax
import jax.numpy as jnp
from jax import lax
from jax.experimental import pallas as pl
from jax.experimental.pallas import tpu as pltpu
from jax.sharding import PartitionSpec as P

HDIM = 128
XS, YLS, ZS = 4, 2, 4
BF16, F32 = jnp.bfloat16, jnp.float32
VMEM = pl.BlockSpec(memory_space=pltpu.VMEM)
SMEM = pl.BlockSpec(memory_space=pltpu.SMEM)
ANY = pl.BlockSpec(memory_space=pl.ANY)
PARAMS = pltpu.CompilerParams(vmem_limit_bytes=20 * 1024 * 1024)
WIDE = pltpu.CompilerParams(vmem_limit_bytes=60 * 1024 * 1024)


def moves(rule):
    pairs = []
    for yh in range(2):
        for core in range(2):
            for x in range(XS):
                for yl in range(YLS):
                    for z in range(ZS):
                        to = rule(yh, core, x, yl, z)
                        if to is not None:
                            pairs.append((flat(yh, core, x, yl, z), flat(*to)))
    return pairs


def flat(yh, core, x, yl, z):
    return (((yh * 2 + core) * XS + x) * YLS + yl) * ZS + z


def send(value, rule):
    return lax.ppermute(value, ("tm", "seq"), moves(rule))


def first_axis(step):
    return lambda yh, core, x, yl, z: (
        (yh, core, (x + step) % XS, yl, z) if core == 0 else (yh, core, x, yl, (z + step) % ZS)
    )


def second_axis(step):
    return lambda yh, core, x, yl, z: (
        (yh, core, x, yl, (z + step) % ZS) if core == 0 else (yh, core, (x + step) % XS, yl, z)
    )


def to_other_core(yh, core, x, yl, z):
    return (yh, 1 - core, x, yl, z)


def to_partner(yh, core, x, yl, z):
    return (yh, core, x, 1 - yl, z)


def to_both_sides(yh, core, x, yl, z):
    return (yh if core == 0 else 1 - yh, core, x, 1 - yl, z)


def to_other_half(yh, core, x, yl, z):
    return (1 - yh, core, x, yl, z)


def modulate_kernel(index, state, scale, shift, gate, out, gates):
    row = pl.ds(lax.rem(index[0], 8), 1)
    value = state[...]
    mean = jnp.mean(value * value, axis=-1, keepdims=True)
    normed = value * lax.rsqrt(mean + 1e-06)
    out[...] = (normed * (1.0 + scale[row, :]) + shift[row, :]).astype(BF16)
    gates[...] = gate[row, :]


def modulate(index, state, scale, shift, gate):
    rows, width = state.shape
    table = pl.BlockSpec((8, width), lambda i, index: (lax.div(index[0], 8), 0))
    whole = pl.BlockSpec((rows, width), lambda i, index: (0, 0))
    return pl.pallas_call(
        modulate_kernel,
        grid_spec=pltpu.PrefetchScalarGridSpec(
            num_scalar_prefetch=1,
            grid=(1,),
            in_specs=[whole, table, table, table],
            out_specs=[whole, pl.BlockSpec((1, width), lambda i, index: (0, 0))],
        ),
        out_shape=[
            jax.ShapeDtypeStruct(state.shape, BF16),
            jax.ShapeDtypeStruct((1, width), F32),
        ],
        compiler_params=WIDE,
        cost_estimate=pl.CostEstimate(flops=1000000, bytes_accessed=2000000, transcendentals=0),
    )(index, state, scale, shift, gate)


def pack_kernel(kinds, core, qkv, *refs):
    packed, sem = refs[-2:]
    half = packed.shape[1]
    first = pl.multiple_of(core[0] * half, half)
    copies = []
    for place, kind in enumerate(kinds):
        if kind < 3:
            rows = qkv.at[kind, pl.ds(first, half), :]
            copies.append(pltpu.make_async_copy(rows, packed.at[place], sem))
        else:
            for at in range(0, half, HDIM):
                block = refs[0].at[:, pl.ds(pl.multiple_of(first + at, HDIM), HDIM)]
                copies.append(
                    pltpu.make_async_copy(block, packed.at[place, pl.ds(at, HDIM), :], sem)
                )
    for copy in copies:
        copy.start()
    for copy in copies:
        copy.wait()


def pack(kinds, core, qkv_weight, *more):
    half = qkv_weight.shape[1] // 2
    return pl.pallas_call(
        functools.partial(pack_kernel, kinds),
        grid_spec=pltpu.PrefetchScalarGridSpec(
            num_scalar_prefetch=1,
            grid=(1,),
            in_specs=[ANY] * (1 + len(more)),
            out_specs=pl.BlockSpec((len(kinds), half, HDIM), lambda i, core: (0, 0, 0)),
            scratch_shapes=[pltpu.SemaphoreType.DMA],
        ),
        out_shape=jax.ShapeDtypeStruct((len(kinds), half, HDIM), BF16),
        compiler_params=PARAMS,
        cost_estimate=pl.CostEstimate(flops=0, bytes_accessed=4000000, transcendentals=0),
    )(core, qkv_weight, *more)


def stack_kernel(*refs):
    out, at = refs[-1], 0
    for piece in refs[:-1]:
        out[at : at + piece.shape[0]] = piece[...]
        at += piece.shape[0]


def stack(*pieces):
    return pl.pallas_call(
        stack_kernel,
        out_shape=jax.ShapeDtypeStruct(
            (sum(piece.shape[0] for piece in pieces), pieces[0].shape[1]), BF16
        ),
        in_specs=[VMEM] * len(pieces),
        out_specs=VMEM,
        compiler_params=PARAMS,
    )(*pieces)


def halves_kernel(one, two, *refs):
    low, high = refs[-2:]
    half = low.shape[0]
    low[...] = one[:half]
    high[...] = two[half:]


def first_and_second_half(one, two, *until):
    return pl.pallas_call(
        halves_kernel,
        out_shape=[jax.ShapeDtypeStruct((one.shape[0] // 2, one.shape[1]), BF16)] * 2,
        in_specs=[VMEM] * 2 + [ANY] * len(until),
        out_specs=[VMEM] * 2,
        compiler_params=PARAMS,
    )(one, two, *until)


def sides(core, mine, theirs, width, step, one):
    half = width // 2
    first = core[0] * half

    def side(weight, start):
        def body(block, carry):
            at = pl.multiple_of(block * step, step)
            one(weight, at, pl.multiple_of(start + at, 128))
            return carry

        lax.fori_loop(0, half // step, body, 0, unroll=True)

    side(mine, first)
    side(theirs, half - first)


def project_kernel(count, kinds, rows, core, *refs):
    pieces, (own, mine, theirs) = refs[:count], refs[count : count + 3]
    outs, total = refs[count + 3 : -1], refs[-1]
    step, wide = 512, 2 * HDIM
    total[...] = jnp.zeros_like(total)

    def one(weight, at, column):
        left = jnp.concatenate([piece[:, pl.ds(column, step)] for piece in pieces], axis=0)
        for place, kind in enumerate(kinds):
            both = jnp.concatenate(
                [own[kind, pl.ds(column, step), :], weight[place, pl.ds(at, step), :]], axis=-1
            )
            total[place] += jnp.dot(left, both, preferred_element_type=F32)

    sides(core, mine, theirs, own.shape[1], step, one)
    at = 0
    for out, size in zip(outs, rows):
        for place in range(len(kinds)):
            out[:, place * wide : (place + 1) * wide] = total[place, at : at + size].astype(BF16)
        at += size


def project(core, kinds, pieces, weight, mine, theirs, rows):
    wide = 2 * HDIM
    tokens, depth = sum(rows), weight.shape[1]
    return pl.pallas_call(
        functools.partial(project_kernel, len(pieces), kinds, rows),
        out_shape=[jax.ShapeDtypeStruct((size, len(kinds) * wide), BF16) for size in rows],
        in_specs=[SMEM] + [VMEM] * (len(pieces) + 3),
        out_specs=[VMEM] * len(rows),
        scratch_shapes=[pltpu.VMEM((len(kinds), tokens, wide), F32)],
        compiler_params=PARAMS,
        cost_estimate=pl.CostEstimate(
            flops=2 * len(kinds) * tokens * depth * wide, bytes_accessed=1000000, transcendentals=0
        ),
    )(core, *pieces, weight, mine, theirs)


def attend_kernel(count, cuts, core, queries, own, mine, theirs, *refs):
    near, far = refs[:count], refs[count : 2 * count]
    outs, attended = refs[2 * count : -1], refs[-1]
    scale = 1.0 / math.sqrt(HDIM)
    contract = (((1,), (1,)), ((), ()))
    for head in range(2):
        here = slice(head * HDIM, (head + 1) * HDIM)
        there = slice((1 - head) * HDIM, (2 - head) * HDIM)
        here_v = slice((2 + head) * HDIM, (3 + head) * HDIM)
        there_v = slice((3 - head) * HDIM, (4 - head) * HDIM)
        all_keys = jnp.concatenate([r[:, here] for r in near] + [r[:, there] for r in far], axis=0)
        all_values = jnp.concatenate(
            [r[:, here_v] for r in near] + [r[:, there_v] for r in far], axis=0
        )
        scores = lax.dot_general(queries[:, here], all_keys, contract, preferred_element_type=F32)
        top = jnp.max(scores, axis=-1, keepdims=True)
        weights = jnp.exp((scores - top) * scale)
        total = jnp.sum(weights, axis=-1, keepdims=True)
        mixed = jnp.dot(weights.astype(BF16), all_values, preferred_element_type=F32)
        attended[:, here] = (mixed / total).astype(BF16)
    step = 512

    def one(weight, at, column):
        blocks = [
            weight[1, pl.ds(pl.multiple_of(at + i, HDIM), HDIM), :] for i in range(0, step, HDIM)
        ]
        both = jnp.concatenate(
            [own[:, pl.ds(column, step)], jnp.concatenate(blocks, axis=1)], axis=0
        )
        result = jnp.dot(attended[...], both, preferred_element_type=F32).astype(BF16)
        row = 0
        for out, size in zip(outs, cuts):
            out[:, pl.ds(column, step)] = result[row : row + size]
            row += size

    sides(core, mine, theirs, own.shape[1], step, one)


def attend(core, queries, near, far, own, mine, theirs, cuts):
    width = own.shape[1]
    tokens = queries.shape[0]
    return pl.pallas_call(
        functools.partial(attend_kernel, len(near), cuts),
        out_shape=[jax.ShapeDtypeStruct((size, width), BF16) for size in cuts],
        in_specs=[SMEM] + [VMEM] * (4 + 2 * len(near)),
        out_specs=[VMEM] * len(cuts),
        scratch_shapes=[pltpu.VMEM((tokens, 2 * HDIM), BF16)],
        compiler_params=PARAMS,
        cost_estimate=pl.CostEstimate(
            flops=4 * tokens * HDIM * (width + 2048), bytes_accessed=1000000, transcendentals=0
        ),
    )(core, queries, own, mine, theirs, *near, *far)


def join_kernel(after, before, low, high, to_after, to_before):
    to_after[...] = (after[...].astype(F32) + low[...].astype(F32)).astype(BF16)
    to_before[...] = (before[...].astype(F32) + high[...].astype(F32)).astype(BF16)


def join(after, before, low, high):
    return pl.pallas_call(
        join_kernel,
        out_shape=[jax.ShapeDtypeStruct(before.shape, BF16)] * 2,
        in_specs=[VMEM] * 4,
        out_specs=[VMEM] * 2,
        compiler_params=PARAMS,
    )(after, before, low, high)


def split_kernel(*refs):
    near_low, near_high, low_1, low_2, high_1, high_2 = refs[:6]
    kept, to_minus, to_plus, to_opposite = refs[-4:]
    size = kept.shape[0]

    def total(near, one, two, rows):
        return near[rows].astype(F32) + one[rows].astype(F32) + two[rows].astype(F32)

    kept[...] = total(near_low, low_1, low_2, slice(0, size))
    to_minus[...] = total(near_low, low_1, low_2, slice(size, 2 * size)).astype(BF16)
    to_plus[...] = total(near_high, high_1, high_2, slice(0, size)).astype(BF16)
    to_opposite[...] = total(near_high, high_1, high_2, slice(size, 2 * size)).astype(BF16)


def split(*parts):
    size, width = parts[0].shape[0] // 2, parts[0].shape[1]
    return pl.pallas_call(
        split_kernel,
        out_shape=[jax.ShapeDtypeStruct((size, width), F32)]
        + [jax.ShapeDtypeStruct((size, width), BF16)] * 3,
        in_specs=[VMEM] * 6,
        out_specs=[VMEM] * 4,
        compiler_params=PARAMS,
    )(*parts)


def drift_kernel(index, steps, total, one, two, three, gates, *refs):
    drift, term = refs[-2:]
    moved = total[...] + one[...].astype(F32) + two[...].astype(F32) + three[...].astype(F32)
    result = steps[index[0]] * (gates[...] * moved)
    drift[...] = result
    term[...] = result.astype(BF16)


def drifts(index, steps, total, arrived, gates, *until):
    return pl.pallas_call(
        drift_kernel,
        out_shape=[
            jax.ShapeDtypeStruct(total.shape, F32),
            jax.ShapeDtypeStruct(total.shape, BF16),
        ],
        in_specs=[SMEM] * 2 + [VMEM] * 5 + [ANY] * len(until),
        out_specs=[VMEM] * 2,
        compiler_params=PARAMS,
    )(index, steps, total, *arrived, gates, *until)


def own_rows(place, half):
    return pl.ds(pl.multiple_of(lax.rem(place[0], 2) * half, half), half)


def start_kernel(place, state, received, until, out):
    rows = own_rows(place, out.shape[0])
    out[...] = jnp.where(place[0] == 0, state[rows, :], received[rows, :])


def start_half(place, state, received, until):
    return pl.pallas_call(
        start_kernel,
        out_shape=jax.ShapeDtypeStruct((state.shape[0] // 2, state.shape[1]), F32),
        in_specs=[SMEM] + [VMEM] * 2 + [ANY],
        out_specs=VMEM,
        compiler_params=PARAMS,
    )(place, state, received, until)


def both_kernel(place, drift, beside, out):
    rows = own_rows(place, out.shape[0])
    out[...] = (drift[rows, :] + beside[rows, :].astype(F32)).astype(BF16)


def both_half(place, drift, beside):
    return pl.pallas_call(
        both_kernel,
        out_shape=jax.ShapeDtypeStruct((drift.shape[0] // 2, drift.shape[1]), BF16),
        in_specs=[SMEM] + [VMEM] * 2,
        out_specs=VMEM,
        compiler_params=PARAMS,
    )(place, drift, beside)


def finish_kernel(place, state, near_start, own_start, far_start, drift, beside, own_sum, far_sum, out):
    half = own_sum.shape[0]
    second = lax.rem(place[0], 2)
    summed = drift[...] + jnp.where(second == 1, beside[...].astype(F32), 0.0)

    @pl.when(place[0] < 2)
    def _():
        out[...] = jnp.where(place[0] == 0, state[...], near_start[...]) + summed

    @pl.when(place[0] >= 2)
    def _():
        for which, start, earlier in ((0, own_start, own_sum), (1, far_start, far_sum)):
            rows = pl.ds(pl.multiple_of(lax.rem(second + which, 2) * half, half), half)
            out[rows, :] = start[...] + earlier[...].astype(F32)
        out[...] += summed


def finish(place, *parts):
    return pl.pallas_call(
        finish_kernel,
        out_shape=jax.ShapeDtypeStruct(parts[0].shape, F32),
        in_specs=[SMEM] + [VMEM] * 8,
        out_specs=VMEM,
        compiler_params=PARAMS,
    )(place, *parts)


def hold_kernel(value, *refs):
    del value, refs


def hold(value, *until):
    return pl.pallas_call(
        hold_kernel,
        out_shape=jax.ShapeDtypeStruct(value.shape, value.dtype),
        in_specs=[ANY] * (1 + len(until)),
        out_specs=ANY,
        input_output_aliases={0: 0},
        compiler_params=PARAMS,
    )(value, *until)


def on_device(
    trajectory, qkv_weight, out_weight, shift_table, scale_table, gate_table, step_sizes, window_start
):
    group = lax.axis_index("tm")
    core = group & 1
    place, core, index = group[None], core[None], window_start + group
    state = trajectory[0]
    modulated, gates = modulate(index, state, scale_table, shift_table, gate_table)
    near_start = send(state, to_other_core)
    minus, plus, opposite = [send(modulated, first_axis(s)) for s in (1, -1, 2)]
    near = stack(modulated, minus, plus, opposite)
    before, after = send(near, second_axis(1)), send(near, second_axis(-1))
    kv_mine = send(pack((1, 2), core, qkv_weight, gates), to_both_sides)
    qo_mine = send(pack((0, 3), core, qkv_weight, out_weight, minus, plus, opposite), to_both_sides)
    before_half, after_half = first_and_second_half(before, after, near_start)
    last = [send(before_half, second_axis(1)), send(after_half, second_axis(-1))]

    size = before_half.shape[0]
    kv_mine = hold(kv_mine, near)
    kv_weights = (qkv_weight, kv_mine, send(kv_mine, to_other_core))
    qo_theirs = send(qo_mine, to_other_core)
    (first_kv,) = project(core, (1, 2), [near, before, after], *kv_weights, [6 * size])
    (last_kv,) = project(core, (1, 2), last, *kv_weights, [2 * size])
    kv = [first_kv, last_kv]
    far = [send(value, to_partner) for value in kv]
    near_q, side_q, last_q = project(
        core,
        (0,),
        [near, before, after, *last],
        qkv_weight,
        qo_mine,
        qo_theirs,
        [2 * size, 4 * size, 2 * size],
    )

    outs = (out_weight, qo_mine, qo_theirs)
    last_low, last_high = attend(core, last_q, kv, far, *outs, [size] * 2)
    own_start = send(start_half(place, state, near_start, last_low), to_other_half)
    from_low, from_high = send(last_low, second_axis(1)), send(last_high, second_axis(-1))
    before_low, before_high, after_low, after_high = attend(
        core, side_q, kv, far, *outs, [size] * 4
    )
    high_1, low_2 = send(after_high, second_axis(1)), send(before_low, second_axis(-1))
    near_low, near_high = attend(core, near_q, kv, far, *outs, [size] * 2)
    after_low, before_high = join(after_low, before_high, from_low, from_high)
    low_1, high_2 = send(after_low, second_axis(1)), send(before_high, second_axis(-1))
    total, to_minus, to_plus, to_opposite = split(
        near_low, near_high, low_1, low_2, high_1, high_2
    )
    arrived = [
        send(value, first_axis(s)) for value, s in ((to_opposite, 2), (to_plus, 1), (to_minus, -1))
    ]
    far_start = send(own_start, to_other_core)
    drift, term = drifts(index, step_sizes, total, arrived, gates, far_start)
    beside = send(term, to_other_core)
    own_sum = send(both_half(place, drift, beside), to_other_half)
    far_sum = send(own_sum, to_other_core)
    return finish(
        place, state, near_start, own_start, far_start, drift, beside, own_sum, far_sum
    )[None]


def solution(mesh):
    in_specs = (P("tm", "seq", None), P(None, None, "seq"), P("seq", None), P(), P(), P(), P(), P())
    out_specs = P("tm", "seq", None)
    return jax.shard_map(
        on_device, mesh=mesh, in_specs=in_specs, out_specs=out_specs, check_vma=False
    )
```

```python
import functools
import math

import jax
import jax.numpy as jnp
from jax import lax
from jax.experimental import pallas as pl
from jax.experimental.pallas import tpu as pltpu
from jax.sharding import PartitionSpec as P

HDIM = 128
XS, YLS, ZS = 4, 2, 4
BF16, F32 = jnp.bfloat16, jnp.float32
VMEM = pl.BlockSpec(memory_space=pltpu.VMEM)
SMEM = pl.BlockSpec(memory_space=pltpu.SMEM)
ANY = pl.BlockSpec(memory_space=pl.ANY)
PARAMS = pltpu.CompilerParams(vmem_limit_bytes=20 * 1024 * 1024)
WIDE = pltpu.CompilerParams(vmem_limit_bytes=60 * 1024 * 1024)


def moves(rule):
    pairs = []
    for yh in range(2):
        for core in range(2):
            for x in range(XS):
                for yl in range(YLS):
                    for z in range(ZS):
                        to = rule(yh, core, x, yl, z)
                        if to is not None:
                            pairs.append((flat(yh, core, x, yl, z), flat(*to)))
    return pairs


def flat(yh, core, x, yl, z):
    return (((yh * 2 + core) * XS + x) * YLS + yl) * ZS + z


def send(value, rule):
    return lax.ppermute(value, ("tm", "seq"), moves(rule))


def first_axis(step):
    return lambda yh, core, x, yl, z: (
        (yh, core, (x + step) % XS, yl, z) if core == 0 else (yh, core, x, yl, (z + step) % ZS)
    )


def second_axis(step):
    return lambda yh, core, x, yl, z: (
        (yh, core, x, yl, (z + step) % ZS) if core == 0 else (yh, core, (x + step) % XS, yl, z)
    )


def to_other_core(yh, core, x, yl, z):
    return (yh, 1 - core, x, yl, z)


def to_partner(yh, core, x, yl, z):
    return (yh, core, x, 1 - yl, z)


def to_both_sides(yh, core, x, yl, z):
    return (yh if core == 0 else 1 - yh, core, x, 1 - yl, z)


def to_other_half(yh, core, x, yl, z):
    return (1 - yh, core, x, yl, z)


def modulate_kernel(index, core, state, scale, shift, gate, out, gates, core_after):
    core_after[0] = core[0]
    row = pl.ds(lax.rem(index[0], 8), 1)
    value = state[...]
    mean = jnp.mean(value * value, axis=-1, keepdims=True)
    normed = value * lax.rsqrt(mean + 1e-06)
    out[...] = (normed * (1.0 + scale[row, :]) + shift[row, :]).astype(BF16)
    gates[...] = gate[row, :]


def modulate(index, core, state, scale, shift, gate):
    rows, width = state.shape
    table = pl.BlockSpec((8, width), lambda i, index, core: (lax.div(index[0], 8), 0))
    whole = pl.BlockSpec((rows, width), lambda i, index, core: (0, 0))
    return pl.pallas_call(
        modulate_kernel,
        grid_spec=pltpu.PrefetchScalarGridSpec(
            num_scalar_prefetch=2,
            grid=(1,),
            in_specs=[whole, table, table, table],
            out_specs=[whole, pl.BlockSpec((1, width), lambda i, index, core: (0, 0)), SMEM],
        ),
        out_shape=[
            jax.ShapeDtypeStruct(state.shape, BF16),
            jax.ShapeDtypeStruct((1, width), F32),
            jax.ShapeDtypeStruct((1,), jnp.int32),
        ],
        compiler_params=WIDE,
        cost_estimate=pl.CostEstimate(flops=1000000, bytes_accessed=2000000, transcendentals=0),
    )(index, core, state, scale, shift, gate)


def pack_kernel(kinds, core, qkv, *refs):
    packed, sem = refs[-2:]
    half = packed.shape[1]
    first = pl.multiple_of(core[0] * half, half)
    copies = []
    for place, kind in enumerate(kinds):
        if kind < 3:
            rows = qkv.at[kind, pl.ds(first, half), :]
            copies.append(pltpu.make_async_copy(rows, packed.at[place], sem))
        else:
            for at in range(0, half, HDIM):
                block = refs[0].at[:, pl.ds(pl.multiple_of(first + at, HDIM), HDIM)]
                copies.append(
                    pltpu.make_async_copy(block, packed.at[place, pl.ds(at, HDIM), :], sem)
                )
    for copy in copies:
        copy.start()
    for copy in copies:
        copy.wait()


def pack(kinds, core, qkv_weight, *more):
    half = qkv_weight.shape[1] // 2
    return pl.pallas_call(
        functools.partial(pack_kernel, kinds),
        grid_spec=pltpu.PrefetchScalarGridSpec(
            num_scalar_prefetch=1,
            grid=(1,),
            in_specs=[ANY] * (1 + len(more)),
            out_specs=pl.BlockSpec((len(kinds), half, HDIM), lambda i, core: (0, 0, 0)),
            scratch_shapes=[pltpu.SemaphoreType.DMA],
        ),
        out_shape=jax.ShapeDtypeStruct((len(kinds), half, HDIM), BF16),
        compiler_params=PARAMS,
        cost_estimate=pl.CostEstimate(flops=0, bytes_accessed=4000000, transcendentals=0),
    )(core, qkv_weight, *more)


def stack_kernel(*refs):
    out, at = refs[-1], 0
    for piece in refs[:-1]:
        out[at : at + piece.shape[0]] = piece[...]
        at += piece.shape[0]


def stack(*pieces):
    return pl.pallas_call(
        stack_kernel,
        out_shape=jax.ShapeDtypeStruct(
            (sum(piece.shape[0] for piece in pieces), pieces[0].shape[1]), BF16
        ),
        in_specs=[VMEM] * len(pieces),
        out_specs=VMEM,
        compiler_params=PARAMS,
    )(*pieces)


def halves_kernel(one, two, *refs):
    low, high = refs[-2:]
    half = low.shape[0]
    low[...] = one[:half]
    high[...] = two[half:]


def first_and_second_half(one, two, *until):
    return pl.pallas_call(
        halves_kernel,
        out_shape=[jax.ShapeDtypeStruct((one.shape[0] // 2, one.shape[1]), BF16)] * 2,
        in_specs=[VMEM] * 2 + [ANY] * len(until),
        out_specs=[VMEM] * 2,
        compiler_params=PARAMS,
    )(one, two, *until)


def sides(core, mine, theirs, width, step, one):
    half = width // 2
    first = core[0] * half

    def side(weight, start):
        def body(block, carry):
            at = pl.multiple_of(block * step, step)
            one(weight, at, pl.multiple_of(start + at, 128))
            return carry

        lax.fori_loop(0, half // step, body, 0, unroll=True)

    side(mine, first)
    side(theirs, half - first)


def project_kernel(count, kinds, rows, core, *refs):
    pieces, (own, mine, theirs) = refs[:count], refs[count : count + 3]
    outs, total = refs[count + 3 : -1], refs[-1]
    step, wide = 512, 2 * HDIM
    total[...] = jnp.zeros_like(total)

    def one(weight, at, column):
        left = jnp.concatenate([piece[:, pl.ds(column, step)] for piece in pieces], axis=0)
        for place, kind in enumerate(kinds):
            both = jnp.concatenate(
                [own[kind, pl.ds(column, step), :], weight[place, pl.ds(at, step), :]], axis=-1
            )
            total[place] += jnp.dot(left, both, preferred_element_type=F32)

    sides(core, mine, theirs, own.shape[1], step, one)
    at = 0
    for out, size in zip(outs, rows):
        for place in range(len(kinds)):
            out[:, place * wide : (place + 1) * wide] = total[place, at : at + size].astype(BF16)
        at += size


def project(core, kinds, pieces, weight, mine, theirs, rows):
    wide = 2 * HDIM
    tokens, depth = sum(rows), weight.shape[1]
    return pl.pallas_call(
        functools.partial(project_kernel, len(pieces), kinds, rows),
        out_shape=[jax.ShapeDtypeStruct((size, len(kinds) * wide), BF16) for size in rows],
        in_specs=[SMEM] + [VMEM] * (len(pieces) + 3),
        out_specs=[VMEM] * len(rows),
        scratch_shapes=[pltpu.VMEM((len(kinds), tokens, wide), F32)],
        compiler_params=PARAMS,
        cost_estimate=pl.CostEstimate(
            flops=2 * len(kinds) * tokens * depth * wide, bytes_accessed=1000000, transcendentals=0
        ),
    )(core, *pieces, weight, mine, theirs)


def attend_kernel(count, cuts, core, queries, own, mine, theirs, *refs):
    near, far = refs[:count], refs[count : 2 * count]
    outs, attended = refs[2 * count : -1], refs[-1]
    scale = 1.0 / math.sqrt(HDIM)
    contract = (((1,), (1,)), ((), ()))
    for head in range(2):
        here = slice(head * HDIM, (head + 1) * HDIM)
        there = slice((1 - head) * HDIM, (2 - head) * HDIM)
        here_v = slice((2 + head) * HDIM, (3 + head) * HDIM)
        there_v = slice((3 - head) * HDIM, (4 - head) * HDIM)
        all_keys = jnp.concatenate([r[:, here] for r in near] + [r[:, there] for r in far], axis=0)
        all_values = jnp.concatenate(
            [r[:, here_v] for r in near] + [r[:, there_v] for r in far], axis=0
        )
        scores = lax.dot_general(queries[:, here], all_keys, contract, preferred_element_type=F32)
        top = jnp.max(scores, axis=-1, keepdims=True)
        weights = jnp.exp((scores - top) * scale)
        total = jnp.sum(weights, axis=-1, keepdims=True)
        mixed = jnp.dot(weights.astype(BF16), all_values, preferred_element_type=F32)
        attended[:, here] = (mixed / total).astype(BF16)
    step = 512

    def one(weight, at, column):
        blocks = [
            weight[1, pl.ds(pl.multiple_of(at + i, HDIM), HDIM), :] for i in range(0, step, HDIM)
        ]
        both = jnp.concatenate(
            [own[:, pl.ds(column, step)], jnp.concatenate(blocks, axis=1)], axis=0
        )
        result = jnp.dot(attended[...], both, preferred_element_type=F32).astype(BF16)
        row = 0
        for out, size in zip(outs, cuts):
            out[:, pl.ds(column, step)] = result[row : row + size]
            row += size

    sides(core, mine, theirs, own.shape[1], step, one)


def attend(core, queries, near, far, own, mine, theirs, cuts):
    width = own.shape[1]
    tokens = queries.shape[0]
    return pl.pallas_call(
        functools.partial(attend_kernel, len(near), cuts),
        out_shape=[jax.ShapeDtypeStruct((size, width), BF16) for size in cuts],
        in_specs=[SMEM] + [VMEM] * (4 + 2 * len(near)),
        out_specs=[VMEM] * len(cuts),
        scratch_shapes=[pltpu.VMEM((tokens, 2 * HDIM), BF16)],
        compiler_params=PARAMS,
        cost_estimate=pl.CostEstimate(
            flops=4 * tokens * HDIM * (width + 2048), bytes_accessed=1000000, transcendentals=0
        ),
    )(core, queries, own, mine, theirs, *near, *far)


def join_kernel(after, before, low, high, to_after, to_before):
    to_after[...] = (after[...].astype(F32) + low[...].astype(F32)).astype(BF16)
    to_before[...] = (before[...].astype(F32) + high[...].astype(F32)).astype(BF16)


def join(after, before, low, high):
    return pl.pallas_call(
        join_kernel,
        out_shape=[jax.ShapeDtypeStruct(before.shape, BF16)] * 2,
        in_specs=[VMEM] * 4,
        out_specs=[VMEM] * 2,
        compiler_params=PARAMS,
    )(after, before, low, high)


def split_kernel(*refs):
    near_low, near_high, low_1, low_2, high_1, high_2 = refs[:6]
    kept, to_minus, to_plus, to_opposite = refs[-4:]
    size = kept.shape[0]

    def total(near, one, two, rows):
        return near[rows].astype(F32) + one[rows].astype(F32) + two[rows].astype(F32)

    kept[...] = total(near_low, low_1, low_2, slice(0, size))
    to_minus[...] = total(near_low, low_1, low_2, slice(size, 2 * size)).astype(BF16)
    to_plus[...] = total(near_high, high_1, high_2, slice(0, size)).astype(BF16)
    to_opposite[...] = total(near_high, high_1, high_2, slice(size, 2 * size)).astype(BF16)


def split(*parts):
    size, width = parts[0].shape[0] // 2, parts[0].shape[1]
    return pl.pallas_call(
        split_kernel,
        out_shape=[jax.ShapeDtypeStruct((size, width), F32)]
        + [jax.ShapeDtypeStruct((size, width), BF16)] * 3,
        in_specs=[VMEM] * 6,
        out_specs=[VMEM] * 4,
        compiler_params=PARAMS,
    )(*parts)


def drift_kernel(index, steps, total, one, two, three, gates, *refs):
    drift, term = refs[-2:]
    moved = total[...] + one[...].astype(F32) + two[...].astype(F32) + three[...].astype(F32)
    result = steps[index[0]] * (gates[...] * moved)
    drift[...] = result
    term[...] = result.astype(BF16)


def drifts(index, steps, total, arrived, gates, *until):
    return pl.pallas_call(
        drift_kernel,
        out_shape=[
            jax.ShapeDtypeStruct(total.shape, F32),
            jax.ShapeDtypeStruct(total.shape, BF16),
        ],
        in_specs=[SMEM] * 2 + [VMEM] * 5 + [ANY] * len(until),
        out_specs=[VMEM] * 2,
        compiler_params=PARAMS,
    )(index, steps, total, *arrived, gates, *until)


def own_rows(place, half):
    return pl.ds(pl.multiple_of(lax.rem(place[0], 2) * half, half), half)


def start_kernel(place, state, received, until, out):
    rows = own_rows(place, out.shape[0])
    out[...] = jnp.where(place[0] == 0, state[rows, :], received[rows, :])


def start_half(place, state, received, until):
    return pl.pallas_call(
        start_kernel,
        out_shape=jax.ShapeDtypeStruct((state.shape[0] // 2, state.shape[1]), F32),
        in_specs=[SMEM] + [VMEM] * 2 + [ANY],
        out_specs=VMEM,
        compiler_params=PARAMS,
    )(place, state, received, until)


def both_kernel(place, drift, beside, out):
    rows = own_rows(place, out.shape[0])
    out[...] = (drift[rows, :] + beside[rows, :].astype(F32)).astype(BF16)


def both_half(place, drift, beside):
    return pl.pallas_call(
        both_kernel,
        out_shape=jax.ShapeDtypeStruct((drift.shape[0] // 2, drift.shape[1]), BF16),
        in_specs=[SMEM] + [VMEM] * 2,
        out_specs=VMEM,
        compiler_params=PARAMS,
    )(place, drift, beside)


def finish_kernel(place, state, near_start, own_start, far_start, drift, beside, own_sum, far_sum, out):
    half = own_sum.shape[0]
    second = lax.rem(place[0], 2)
    summed = drift[...] + jnp.where(second == 1, beside[...].astype(F32), 0.0)

    @pl.when(place[0] < 2)
    def _():
        out[...] = jnp.where(place[0] == 0, state[...], near_start[...]) + summed

    @pl.when(place[0] >= 2)
    def _():
        for which, start, earlier in ((0, own_start, own_sum), (1, far_start, far_sum)):
            rows = pl.ds(pl.multiple_of(lax.rem(second + which, 2) * half, half), half)
            out[rows, :] = start[...] + earlier[...].astype(F32)
        out[...] += summed


def finish(place, *parts):
    return pl.pallas_call(
        finish_kernel,
        out_shape=jax.ShapeDtypeStruct(parts[0].shape, F32),
        in_specs=[SMEM] + [VMEM] * 8,
        out_specs=VMEM,
        compiler_params=PARAMS,
    )(place, *parts)


def hold_kernel(value, *refs):
    del value, refs


def hold(value, *until):
    return pl.pallas_call(
        hold_kernel,
        out_shape=jax.ShapeDtypeStruct(value.shape, value.dtype),
        in_specs=[ANY] * (1 + len(until)),
        out_specs=ANY,
        input_output_aliases={0: 0},
        compiler_params=PARAMS,
    )(value, *until)


def on_device(
    trajectory, qkv_weight, out_weight, shift_table, scale_table, gate_table, step_sizes, window_start
):
    group = lax.axis_index("tm")
    core = group & 1
    place, core, index = group[None], core[None], window_start + group
    state = trajectory[0]
    modulated, gates, core_after = modulate(
        index, core, state, scale_table, shift_table, gate_table
    )
    near_start = send(state, to_other_core)
    minus, plus, opposite = [send(modulated, first_axis(s)) for s in (1, -1, 2)]
    near = stack(modulated, minus, plus, opposite)
    before, after = send(near, second_axis(1)), send(near, second_axis(-1))
    kv_mine = send(pack((1, 2), core_after, qkv_weight), to_both_sides)
    qo_mine = send(pack((0, 3), core, qkv_weight, out_weight, minus, plus, opposite), to_both_sides)
    before_half, after_half = first_and_second_half(before, after, near_start)
    last = [send(before_half, second_axis(1)), send(after_half, second_axis(-1))]

    size = before_half.shape[0]
    kv_mine = hold(kv_mine, near)
    kv_weights = (qkv_weight, kv_mine, send(kv_mine, to_other_core))
    qo_theirs = send(qo_mine, to_other_core)
    (first_kv,) = project(core, (1, 2), [near, before, after], *kv_weights, [6 * size])
    (last_kv,) = project(core, (1, 2), last, *kv_weights, [2 * size])
    kv = [first_kv, last_kv]
    far = [send(value, to_partner) for value in kv]
    near_q, side_q, last_q = project(
        core,
        (0,),
        [near, before, after, *last],
        qkv_weight,
        qo_mine,
        qo_theirs,
        [2 * size, 4 * size, 2 * size],
    )

    outs = (out_weight, qo_mine, qo_theirs)
    last_low, last_high = attend(core, last_q, kv, far, *outs, [size] * 2)
    own_start = send(start_half(place, state, near_start, last_low), to_other_half)
    from_low, from_high = send(last_low, second_axis(1)), send(last_high, second_axis(-1))
    before_low, before_high, after_low, after_high = attend(
        core, side_q, kv, far, *outs, [size] * 4
    )
    high_1, low_2 = send(after_high, second_axis(1)), send(before_low, second_axis(-1))
    near_low, near_high = attend(core, near_q, kv, far, *outs, [size] * 2)
    after_low, before_high = join(after_low, before_high, from_low, from_high)
    low_1, high_2 = send(after_low, second_axis(1)), send(before_high, second_axis(-1))
    total, to_minus, to_plus, to_opposite = split(
        near_low, near_high, low_1, low_2, high_1, high_2
    )
    arrived = [
        send(value, first_axis(s)) for value, s in ((to_opposite, 2), (to_plus, 1), (to_minus, -1))
    ]
    far_start = send(own_start, to_other_core)
    drift, term = drifts(index, step_sizes, total, arrived, gates, far_start)
    beside = send(term, to_other_core)
    own_sum = send(both_half(place, drift, beside), to_other_half)
    far_sum = send(own_sum, to_other_core)
    return finish(
        place, state, near_start, own_start, far_start, drift, beside, own_sum, far_sum
    )[None]


def solution(mesh):
    in_specs = (P("tm", "seq", None), P(None, None, "seq"), P("seq", None), P(), P(), P(), P(), P())
    out_specs = P("tm", "seq", None)
    return jax.shard_map(
        on_device, mesh=mesh, in_specs=in_specs, out_specs=out_specs, check_vma=False
    )
```
